512 devices in a mesh: tm: 64 (over x, z, core), region: 8 (over y).
Axes of the slice: x: 4, y: 8, z: 8, core: 2. Of those that a mesh axis runs over, the one named last changes fastest.
Arguments:
- activity: bfloat16 [6144, 131072], P('region', 'tm'), may hold values from -6 to 6
- test_matrix: bfloat16 [131072, 512], P('tm', 'region'), may hold values from -0.015625 to 0.015625
- basis_mix: float32 [512, 64], replicated, may hold values from -0.25 to 0.25
- recurrent: float32 [64, 64], replicated, may hold values from -0.75 to 0.75
- latent_bias: float32 [64], replicated, may hold values from -2 to 2
- readout: bfloat16 [6144, 64], P('region'), may hold values from -0.75 to 0.75
- region_in: bfloat16 [6144, 8], P('region'), may hold values from -0.21875 to 0.21875
- region_out: bfloat16 [6144, 8], P('region'), may hold values from -1 to 1
- region_of_block: int32 [48], replicated, may hold values from 0 to 7, never falling along the last dimension, each value on 1 to 12 neighbouring positions
- region_mask: int32 [8, 8], replicated, may hold values 0 or 1
Outputs:
- latents: float32 [64, 131072], P(None, 'tm')
- frame_loss: float32 [131072], P('tm')
- readout_score: float32 [6144, 64], P('region')
The draws below stay inside these ranges and needn't reach their ends.
Inputs may be any that keep to these rules, and one draw needn't show every extreme that they name: `region_of_block`: blocks of one region are consecutive, every region holds at least one block, and no region holds more than 12 blocks.
All inputs are finite; a program needn't handle non-finite values.
Results may differ from the reference program's by a relative error of at most 0.0028.
Values may be sent and summed in bfloat16 or wider, within the bound.
No kernel may reach another device: no remote copies, remote signals or barrier semaphores. Data moves between devices by JAX's collectives and lax.ppermute only.
A program may use at most 64 MiB of HBM per device.

```python
import math
import jax
import jax.numpy as jnp
import numpy as np
from jax import lax

NEU_DEV = 768
FR_DEV = 2048
SK = 512
RANK = 64
KR = 8
NREG = 8
NEURONS = 6144
FRAMES = 131072
NBLOCKS = 48
N_TM = 64
N_REGION = 8


def place_ends(values, own_key, low, largest):
    extent = values.shape
    place = [jax.random.randint(jax.random.fold_in(own_key, axis), (), 0, extent[axis]) for axis in range(len(extent))]
    values = values.at[tuple(place)].set(low)
    longest = extent.index(max(extent))
    place[longest] = (place[longest] + 1) % extent[longest]
    return values.at[tuple(place)].set(largest)


def steps_of(rng, extent, shards, low, largest):
    def one(axis_at, parts):
        draws = jax.random.uniform(jax.random.fold_in(jax.random.fold_in(rng, 6), axis_at), (parts,), jnp.float32, low / len(shards), largest / len(shards))
        return jnp.repeat(jnp.exp(draws), extent[axis_at] // parts).reshape((-1,) + (1,) * (len(extent) - axis_at - 1))

    loudness = one(*shards[0])
    for cut in shards[1:]:
        loudness = loudness * one(*cut)
    return loudness


def split_up(amount, total, reach, skew):
    weights = [(1 << 20) // math.isqrt(rank ** skew) + 1 for rank in range(2, amount + 1)]
    spare, counts = total - reach - (amount - 1), [1] * (amount - 1)
    while spare > 0:
        candidates = [i for i in range(amount - 1) if counts[i] < reach]
        whole, remaining = sum([weights[i] for i in candidates]), spare
        for i in candidates:
            addition = min(reach - counts[i], max(1, remaining * weights[i] // whole), spare)
            counts[i] = counts[i] + addition
            spare = spare - addition
    return np.array([reach] + counts)


def ragged_sizes(stream_key, count, total, bound, slope):
    if count == 2:
        one = jax.random.randint(stream_key, (), max(1, total - bound), min(bound, total - 1) + 1)
        return jnp.stack([one, total - one])
    sizes = jnp.asarray(split_up(count, total, bound, slope), jnp.int32)
    pairs = (count - 1) // 2
    donor, sink = sizes[1:1 + 2 * pairs:2], sizes[2:2 + 2 * pairs:2]
    margin = jnp.minimum(donor - 1, bound - sink)
    shifted = jax.random.randint(jax.random.fold_in(stream_key, 1), (pairs,), 0, 1 << 20) % (margin + 1)
    sizes = sizes.at[1:1 + 2 * pairs:2].set(donor - shifted).at[2:2 + 2 * pairs:2].set(sink + shifted)
    return sizes[jax.random.permutation(jax.random.fold_in(stream_key, 2), count)]


def normal_values(key, extent, scale, reach, shards=(), kind=jnp.bfloat16):
    values = scale * jax.random.normal(key, extent, jnp.float32)
    if shards:
        values = values * steps_of(key, extent, shards, -0.22, 0.18)
    return jnp.clip(values, -reach, reach).astype(kind)


def setup_inputs(seed: int = 0) -> dict:
    arg_keys = jax.random.split(jax.random.key(seed), 11)
    activity = normal_values(arg_keys[0], (NEURONS, FRAMES), 1.0, 6.0, ((0, 8), (1, 64)))
    test_matrix = normal_values(arg_keys[1], (FRAMES, SK), FRAMES ** -0.5, 0.015625, ((0, 64), (1, 8)))
    basis_mix = normal_values(arg_keys[2], (SK, RANK), SK ** -0.5, 0.25, (), jnp.float32)
    recurrent = normal_values(arg_keys[3], (RANK, RANK), RANK ** -0.5, 0.75, (), jnp.float32)
    latent_bias = normal_values(arg_keys[4], (RANK,), 0.5, 2.0, (), jnp.float32)
    readout = normal_values(arg_keys[5], (NEURONS, RANK), RANK ** -0.5, 0.75, ((0, 8),))
    region_in = normal_values(arg_keys[6], (NEURONS, KR), (NEU_DEV * N_REGION // NREG) ** -0.5, 0.21875, ((0, 8),))
    region_out = normal_values(arg_keys[7], (NEURONS, KR), (NREG * KR // 2) ** -0.5, 1.0, ((0, 8),))
    region_of_block = jnp.searchsorted(jnp.cumsum(ragged_sizes(arg_keys[8], NREG, NBLOCKS, max(2, NBLOCKS // 4), 2)), jnp.arange(NBLOCKS), side="right").astype(jnp.int32)
    region_mask = place_ends((jax.random.randint(arg_keys[9], (NREG, NREG), 0, 2) < 1).astype(jnp.int32), jax.random.fold_in(arg_keys[9], 1), 0, 1)
    return {"activity": activity, "test_matrix": test_matrix, "basis_mix": basis_mix, "recurrent": recurrent, "latent_bias": latent_bias, "readout": readout, "region_in": region_in, "region_out": region_out, "region_of_block": region_of_block, "region_mask": region_mask}


precise = lax.Precision.HIGHEST
epsilon = 1e-05

def orthonormal(sketch, gram):
    lower = jnp.linalg.cholesky(gram)
    return jax.scipy.linalg.solve_triangular(lower, sketch.T, lower=True).T

def region_tables(block_regions, region_mask, region_in, region_out):
    regions = region_mask.shape[0]
    signal_width = region_in.shape[1]
    block_total = block_regions.shape[0]
    block_rows = region_in.shape[0] // block_total
    onehot = (block_regions[:, None] == jnp.arange(regions, dtype=jnp.int32)[None, :]).astype(jnp.float32)
    onehot = jnp.broadcast_to(onehot[:, None, :], (block_total, block_rows, regions)).reshape(block_total * block_rows, regions)
    allowed = jnp.dot(onehot, region_mask.astype(jnp.float32), precision=precise)
    region_feed = (onehot[:, :, None] * region_in.astype(jnp.float32)[:, None, :]).reshape(-1, regions * signal_width)
    spread = (allowed[:, :, None] * region_out.astype(jnp.float32)[:, None, :]).reshape(-1, regions * signal_width)
    return (region_feed.astype(jnp.bfloat16), spread.astype(jnp.bfloat16))

def reference(activity, test_matrix, basis_mix, recurrent, latent_bias, readout, region_in, region_out, region_of_block, region_mask):
    contract = (((0,), (0,)), ((), ()))
    sketch = jnp.dot(activity.astype(jnp.float32), test_matrix.astype(jnp.float32), preferred_element_type=jnp.float32)
    gram = jnp.dot(sketch.T, sketch, precision=precise)
    loading = jnp.dot(orthonormal(sketch, gram), basis_mix, precision=precise).astype(jnp.bfloat16)
    region_feed, spread = region_tables(region_of_block, region_mask, region_in, region_out)
    latents = lax.dot_general(loading.astype(jnp.float32), activity.astype(jnp.float32), contract, preferred_element_type=jnp.float32)
    signals = lax.dot_general(region_feed.astype(jnp.float32), activity.astype(jnp.float32), contract, preferred_element_type=jnp.float32)
    lagged_latents = jnp.concatenate([jnp.zeros((latents.shape[0], 1), jnp.float32), latents[:, :-1]], axis=1)
    lagged_signals = jnp.concatenate([jnp.zeros((signals.shape[0], 1), jnp.float32), signals[:, :-1]], axis=1)
    hidden = jnp.tanh(jnp.dot(recurrent, lagged_latents, precision=precise) + latent_bias[:, None])

    def one_block(running, index):
        offset = (index * FR_DEV).astype(jnp.int32)
        acts = lax.dynamic_slice_in_dim(activity, offset, FR_DEV, 1)
        hid_block = lax.dynamic_slice_in_dim(hidden, offset, FR_DEV, 1)
        sig_block = lax.dynamic_slice_in_dim(lagged_signals, offset, FR_DEV, 1)
        predicted = jnp.dot(readout.astype(jnp.float32), hid_block.astype(jnp.bfloat16).astype(jnp.float32), preferred_element_type=jnp.float32)
        predicted = predicted + jnp.dot(spread.astype(jnp.float32), sig_block.astype(jnp.bfloat16).astype(jnp.float32), preferred_element_type=jnp.float32)
        error = acts.astype(jnp.float32) - predicted
        cross, error_sq = running
        cross = cross + jnp.dot(error, hid_block.T, precision=precise)
        error_sq = error_sq + lax.optimization_barrier(jnp.sum(error * error, axis=1))
        return ((cross, error_sq), lax.optimization_barrier(jnp.sum(error * error, axis=0)))
    start_state = (jnp.zeros((NEURONS, RANK), jnp.float32), jnp.zeros((NEURONS,), jnp.float32))
    (cross, error_sq), frame_sq = lax.scan(one_block, start_state, jnp.arange(N_TM, dtype=jnp.int32))
    hidden_sq = lax.optimization_barrier(jnp.sum(hidden * hidden, axis=1))
    frame_loss = frame_sq.reshape(-1) / NEURONS
    readout_score = cross / jnp.sqrt(FRAMES * (error_sq[:, None] / FRAMES + epsilon) * (hidden_sq[None, :] / FRAMES + epsilon))
    return (latents, frame_loss, readout_score)
```

```python
import functools

import jax
import jax.numpy as jnp
from jax import lax
from jax.experimental import pallas as pl
from jax.experimental.pallas import tpu as pltpu
from jax.sharding import Mesh
from jax.sharding import PartitionSpec as P

BLOCK = 128
CORES = 2
SLAB = ("chip", "core")

precise = lax.Precision.HIGHEST
epsilon = 1e-05
full = jnp.float32
half = jnp.bfloat16


def product(a, b, ca, cb, precision=None):
    return lax.dot_general(
        a, b, (((ca,), (cb,)), ((), ())), precision=precision, preferred_element_type=full
    )


def other_core(x):
    return lax.ppermute(x, "core", [(0, 1), (1, 0)])


def scatter_sum(pieces, axis):
    return jnp.sum(lax.all_to_all(pieces, axis, 0, 0), axis=0)


def share(x, axis):
    copies = jnp.broadcast_to(x[None], (lax.axis_size(axis),) + x.shape)
    return lax.all_to_all(lax.optimization_barrier(copies), axis, 0, 0)


def in_core_order(mine, theirs):
    first = lax.axis_index("core") == 0
    return jnp.where(first, mine, theirs), jnp.where(first, theirs, mine)


def inverse_factor(tile):
    n = tile.shape[0]
    groups = n // 8
    sub = lax.broadcasted_iota(jnp.int32, (8, n), 0)
    lane = lax.broadcasted_iota(jnp.int32, (8, n), 1)

    def column(x, j):
        return jnp.broadcast_to(x[:, j : j + 1], x.shape)

    def row(x, j):
        return jnp.broadcast_to(x[j : j + 1, :], x.shape)

    left = [tile[8 * q : 8 * q + 8, :] for q in range(groups)]
    right = [jnp.where(lane == sub + 8 * q, full(1), full(0)) for q in range(groups)]
    for p in range(groups):
        at = [column(left[p], 8 * p + j) for j in range(8)]
        lp, rp = left[p], right[p]
        pivots = jnp.ones_like(lp)
        inverse, left_rows, right_rows, pivot_rows = [], [], [], []
        for j in range(8):
            pivot = row(at[j], j)
            pivots = jnp.where(sub == j, pivot, pivots)
            inverse.append(1.0 / pivot)
            left_rows.append(row(lp, j))
            right_rows.append(row(rp, j))
            pivot_rows.append([row(at[k], j) for k in range(j + 1, 8)])
            if j < 7:
                factor = jnp.where(sub > j, at[j] * inverse[j], 0.0)
                for k in range(j + 1, 8):
                    at[k] = at[k] - factor * pivot_rows[j][k - j - 1]
                lp = lp - factor * left_rows[j]
                rp = rp - factor * right_rows[j]
        right[p] = rp * lax.rsqrt(pivots)
        for q in range(p + 1, groups):
            at = [column(left[q], 8 * p + j) for j in range(8)]
            lq, rq = left[q], right[q]
            for j in range(8):
                factor = at[j] * inverse[j]
                for k in range(j + 1, 8):
                    at[k] = at[k] - factor * pivot_rows[j][k - j - 1]
                lq = lq - factor * left_rows[j]
                rq = rq - factor * right_rows[j]
            left[q], right[q] = lq, rq
    return jnp.concatenate(right, axis=0)


def latents_kernel(
    gram_low, gram_high, sketch_low, sketch_high, mix, before, activity, out, work, inverse, weights
):
    n = work.shape[0]
    mid = n // 2
    work[:mid, :] = gram_low[...]
    work[mid:, :] = gram_high[...]
    starts = range(0, n, BLOCK)
    for a in starts:
        e = a + BLOCK
        inverse[a:e, :] = inverse_factor(work[a:e, a:e])
        if e < n:
            below = product(work[e:, a:e], inverse[a:e, :], 1, 1, precise)
            work[e:, a:e] = below
            work[e:, e:] = work[e:, e:] - product(below, below, 1, 1, precise)
    for a in reversed(starts):
        e = a + BLOCK
        rest = mix[:, a:e]
        if e < n:
            rest = rest - product(weights[:, e:], work[e:, a:e], 1, 0, precise)
        weights[:, a:e] = product(rest, inverse[a:e, :], 1, 0, precise)
    loading = product(weights[:, :mid], sketch_low[...], 1, 0, precise)
    loading = loading + product(weights[:, mid:], sketch_high[...], 1, 0, precise)
    loading = loading.astype(half)
    rank = loading.shape[0]
    pieces, rows, width = out.shape
    prior = product(before[...], loading, 1, 1)
    for i in range(pieces):
        out[i, :rank, :] = product(
            loading, activity[:, i * width : (i + 1) * width], 1, 0
        )
        out[i, rank:, :] = jnp.zeros((rows - rank, width), full)
        out[i, rank:, :rank] = prior[: rows - rank, :]


def in_vmem(count):
    return [pl.BlockSpec(memory_space=pltpu.VMEM)] * count


def latent_parts(gram, sketch, mix, before, activity, pieces):
    n = mix.shape[1]
    rank = mix.shape[0]
    frames = activity.shape[1]
    return pl.pallas_call(
        latents_kernel,
        out_shape=jax.ShapeDtypeStruct((pieces, rank + 8, frames // pieces), full),
        in_specs=in_vmem(7),
        out_specs=in_vmem(1)[0],
        scratch_shapes=[
            pltpu.VMEM((n, n), full),
            pltpu.VMEM((n, BLOCK), full),
            pltpu.VMEM((rank, n), full),
        ],
        compiler_params=pltpu.CompilerParams(vmem_limit_bytes=40 * 2**20),
        cost_estimate=pl.CostEstimate(
            flops=2 * n**3, bytes_accessed=8 * 2**20, transcendentals=n
        ),
        name="latent_parts",
    )(*gram, *sketch, mix, before, activity)


def lag(block, carry):
    lane = lax.broadcasted_iota(jnp.int32, block.shape, 1)
    return jnp.where(lane == 0, carry, pltpu.roll(block, 1, 1))


def as_column(line):
    n = line.shape[1]
    square = (n, n)
    same = lax.broadcasted_iota(jnp.int32, square, 0) == lax.broadcasted_iota(jnp.int32, square, 1)
    return jnp.sum(jnp.where(same, line, 0.0), axis=1, keepdims=True)


def error_kernel(
    latents, signals, activity, maps, recurrent, bias,
    latents_out, frame_out, stats,
    last_latent, last_signal, cross, squares, hidden_squares,
):
    i = pl.program_id(0)
    rank = recurrent.shape[0]
    width = activity.shape[1]
    neurons = activity.shape[0]

    @pl.when(i == 0)
    def _():
        wide = last_latent.shape
        last_latent[...] = jnp.broadcast_to(as_column(latents[0, rank : rank + 1, :rank]), wide)
        last_signal[...] = jnp.broadcast_to(as_column(signals[0, rank : rank + 1, :rank]), wide)
        cross[...] = jnp.zeros_like(cross)
        squares[...] = jnp.zeros_like(squares)
        hidden_squares[...] = jnp.zeros_like(hidden_squares)

    latent = latents[0, :rank, :]
    signal = signals[0, :rank, :]
    latents_out[...] = latent
    lagged_latent = lag(latent, last_latent[:, :1])
    lagged_signal = lag(signal, last_signal[:, :1])
    last_latent[...] = jnp.broadcast_to(latent[:, width - 1 :], last_latent.shape)
    last_signal[...] = jnp.broadcast_to(signal[:, width - 1 :], last_signal.shape)
    hidden = jnp.tanh(product(recurrent[...], lagged_latent, 1, 0, precise) + bias[...])
    state = jnp.concatenate([hidden.astype(half), lagged_signal.astype(half)], axis=0)
    error = activity[...].astype(full) - product(maps[...], state, 1, 0)
    squared = error * error
    cross[...] += product(hidden, error, 1, 1, precise)
    frame_out[...] = jnp.sum(squared, axis=0, keepdims=True)
    total = squared[:, :BLOCK]
    hidden_square = hidden * hidden
    hidden_total = hidden_square[:, :BLOCK]
    for a in range(BLOCK, width, BLOCK):
        total = total + squared[:, a : a + BLOCK]
        hidden_total = hidden_total + hidden_square[:, a : a + BLOCK]
    squares[...] += total
    hidden_squares[...] += hidden_total

    @pl.when(i == pl.num_programs(0) - 1)
    def _():
        groups = neurons // BLOCK
        error_sq = product(jnp.ones((8, BLOCK), full), squares[...], 1, 1, precise)
        hidden_sq = jnp.sum(hidden_squares[...], axis=1, keepdims=True)
        stats[...] = jnp.zeros_like(stats)
        for g in range(groups):
            lanes = slice(g * BLOCK, (g + 1) * BLOCK)
            stats[:, g, :] = cross[:, lanes]
            stats[g, groups + 1 : groups + 2, :] = error_sq[:1, lanes]
        stats[:, groups, :] = jnp.broadcast_to(hidden_sq, (rank, BLOCK))


def error_stats(latents, signals, activity, maps, recurrent, bias):
    pieces, rows, width = latents.shape
    neurons, frames = activity.shape
    rank = recurrent.shape[0]
    whole = lambda i: (0, 0)
    return pl.pallas_call(
        error_kernel,
        grid=(pieces,),
        out_shape=(
            jax.ShapeDtypeStruct((rank, frames), full),
            jax.ShapeDtypeStruct((1, frames), full),
            jax.ShapeDtypeStruct((rank, neurons // BLOCK + 2, BLOCK), full),
        ),
        in_specs=[
            pl.BlockSpec((1, rows, width), lambda i: (i, 0, 0)),
            pl.BlockSpec((1, rows, width), lambda i: (i, 0, 0)),
            pl.BlockSpec((neurons, width), lambda i: (0, i)),
            pl.BlockSpec(maps.shape, whole),
            pl.BlockSpec(recurrent.shape, whole),
            pl.BlockSpec(bias.shape, whole),
        ],
        out_specs=(
            pl.BlockSpec((rank, width), lambda i: (0, i)),
            pl.BlockSpec((1, width), lambda i: (0, i)),
            pl.BlockSpec((rank, neurons // BLOCK + 2, BLOCK), lambda i: (0, 0, 0)),
        ),
        scratch_shapes=[
            pltpu.VMEM((rank, BLOCK), full),
            pltpu.VMEM((rank, BLOCK), full),
            pltpu.VMEM((rank, neurons), full),
            pltpu.VMEM((neurons, BLOCK), full),
            pltpu.VMEM((rank, BLOCK), full),
        ],
        compiler_params=pltpu.CompilerParams(vmem_limit_bytes=40 * 2**20),
        cost_estimate=pl.CostEstimate(
            flops=8 * neurons * frames * rank, bytes_accessed=8 * 2**20, transcendentals=rank * frames
        ),
        name="error_stats",
    )(latents, signals, activity, maps, recurrent, bias)


def score_kernel(frames_all, stats, out):
    groups = stats.shape[1] - 2
    hidden_sq = stats[:, groups, :]
    for g in range(groups):
        lanes = slice(g * BLOCK, (g + 1) * BLOCK)
        error_sq = stats[g, groups + 1 : groups + 2, :]
        out[:, lanes] = stats[:, g, :] / jnp.sqrt(
            frames_all * (error_sq / frames_all + epsilon) * (hidden_sq / frames_all + epsilon)
        )


def scores(stats, frames_all):
    rank, rows, _ = stats.shape
    return pl.pallas_call(
        functools.partial(score_kernel, float(frames_all)),
        out_shape=jax.ShapeDtypeStruct((rank, (rows - 2) * BLOCK), full),
        in_specs=in_vmem(1),
        out_specs=in_vmem(1)[0],
        name="scores",
    )(stats)


def region_tables(block_regions, region_mask, region_in, region_out):
    regions = region_mask.shape[0]
    signal_width = region_in.shape[1]
    block_total = block_regions.shape[0]
    block_rows = region_in.shape[0] // block_total
    onehot = (block_regions[:, None] == jnp.arange(regions, dtype=jnp.int32)[None, :]).astype(full)
    onehot = jnp.broadcast_to(onehot[:, None, :], (block_total, block_rows, regions)).reshape(
        block_total * block_rows, regions
    )
    allowed = jnp.dot(onehot, region_mask.astype(full), precision=precise)
    region_feed = (onehot[:, :, None] * region_in.astype(full)[:, None, :]).reshape(
        -1, regions * signal_width
    )
    spread = (allowed[:, :, None] * region_out.astype(full)[:, None, :]).reshape(
        -1, regions * signal_width
    )
    return (region_feed.astype(half), spread.astype(half))


def local(
    activity,
    test_matrix,
    basis_mix,
    recurrent,
    latent_bias,
    readout,
    region_in,
    region_out,
    region_of_block,
    region_mask,
):
    neurons_here, frames_here = activity.shape
    columns = test_matrix.shape[1] * lax.axis_size("region")
    chips = lax.axis_size("chip")
    slabs = chips * CORES
    regions = lax.axis_size("region")
    core = lax.axis_index("core")

    test_full = lax.all_gather(test_matrix.T, "region", axis=0, tiled=True)
    before = lax.ppermute(activity[:, -1], SLAB, [(i, i + 1) for i in range(slabs - 1)])
    before = jnp.broadcast_to(before[None, :], (16, neurons_here))

    block_count = neurons_here // BLOCK
    my_blocks = lax.dynamic_slice_in_dim(
        region_of_block, lax.axis_index("region") * block_count, block_count
    )
    region_feed, spread = region_tables(my_blocks, region_mask, region_in, region_out)
    maps = jnp.concatenate([readout, spread], axis=1)
    rank = region_feed.shape[1]
    signal = product(region_feed, activity, 0, 0)
    signal = signal.reshape(rank, regions, -1).transpose(1, 0, 2)
    prior = jnp.pad(product(before[:8], region_feed, 1, 0), ((0, 0), (0, signal.shape[2] - rank)))
    prior = jnp.broadcast_to(prior[None], (regions,) + prior.shape)
    signal = jnp.concatenate([signal, prior], axis=1)
    signal, test_full = lax.optimization_barrier((signal, test_full))
    signals = lax.psum(signal, "region")

    mid = columns // CORES
    theirs = product(lax.dynamic_slice_in_dim(test_full, (1 - core) * mid, mid), activity, 1, 1)
    mine = product(lax.dynamic_slice_in_dim(test_full, core * mid, mid), activity, 1, 1)
    mine = mine + other_core(theirs)
    own = scatter_sum(mine.reshape(chips, mid // chips, neurons_here), "chip")
    mine = share(own, "chip").reshape(mid, neurons_here)
    sketch = in_core_order(mine, other_core(mine))

    rows = jnp.concatenate([product(own, part, 1, 1, precise) for part in sketch], axis=1)
    rows = jnp.sum(share(rows, "region"), axis=0)
    mine = share(rows, "chip").reshape(mid, columns)
    gram = in_core_order(mine, other_core(mine))

    parts = latent_parts(gram, sketch, basis_mix.T, before, activity, regions)
    latents = share(scatter_sum(parts, "region"), "region")
    latents_out, frame_sq, stats = error_stats(
        latents, signals, activity, maps, recurrent, latent_bias[:, None]
    )
    frame_sq = lax.psum(frame_sq.reshape(frames_here), "region")
    stats = stats.reshape((slabs, rank // slabs) + stats.shape[1:])
    stats = share(scatter_sum(stats, SLAB), SLAB)
    stats = stats.reshape((rank,) + stats.shape[2:])
    score = scores(stats, frames_here * slabs)
    return (latents_out, frame_sq / (neurons_here * regions), score.T)


def solution(mesh):
    slabs, regions = mesh.devices.shape
    devices = mesh.devices.reshape(slabs // CORES, CORES, regions)
    mesh = Mesh(devices, ("chip", "core", "region"))
    in_specs = (
        P("region", SLAB),
        P(SLAB, "region"),
        P(),
        P(),
        P(),
        P("region", None),
        P("region", None),
        P("region", None),
        P(),
        P(),
    )
    out_specs = (P(None, SLAB), P(SLAB), P("region", None))
    return jax.shard_map(local, mesh=mesh, in_specs=in_specs, out_specs=out_specs, check_vma=False)
```

```python
import functools

import jax
import jax.numpy as jnp
from jax import lax
from jax.experimental import pallas as pl
from jax.experimental.pallas import tpu as pltpu
from jax.sharding import Mesh
from jax.sharding import PartitionSpec as P

BLOCK = 128
CORES = 2
SLAB = ("chip", "core")

precise = lax.Precision.HIGHEST
epsilon = 1e-05
full = jnp.float32
half = jnp.bfloat16


def product(a, b, ca, cb, precision=None):
    return lax.dot_general(
        a, b, (((ca,), (cb,)), ((), ())), precision=precision, preferred_element_type=full
    )


def other_core(x):
    return lax.ppermute(x, "core", [(0, 1), (1, 0)])


def scatter_sum(pieces, axis):
    return jnp.sum(lax.all_to_all(pieces, axis, 0, 0), axis=0)


def share(x, axis):
    copies = jnp.broadcast_to(x[None], (lax.axis_size(axis),) + x.shape)
    return lax.all_to_all(lax.optimization_barrier(copies), axis, 0, 0)


def in_core_order(mine, theirs):
    first = lax.axis_index("core") == 0
    return jnp.where(first, mine, theirs), jnp.where(first, theirs, mine)


def inverse_factor(tile):
    n = tile.shape[0]
    groups = n // 8
    sub = lax.broadcasted_iota(jnp.int32, (8, n), 0)
    lane = lax.broadcasted_iota(jnp.int32, (8, n), 1)

    def column(x, j):
        return jnp.broadcast_to(x[:, j : j + 1], x.shape)

    def row(x, j):
        return jnp.broadcast_to(x[j : j + 1, :], x.shape)

    left = [tile[8 * q : 8 * q + 8, :] for q in range(groups)]
    right = [jnp.where(lane == sub + 8 * q, full(1), full(0)) for q in range(groups)]
    for p in range(groups):
        at = [column(left[p], 8 * p + j) for j in range(8)]
        lp, rp = left[p], right[p]
        pivots = jnp.ones_like(lp)
        inverse, left_rows, right_rows, pivot_rows = [], [], [], []
        for j in range(8):
            pivot = row(at[j], j)
            pivots = jnp.where(sub == j, pivot, pivots)
            inverse.append(1.0 / pivot)
            left_rows.append(row(lp, j))
            right_rows.append(row(rp, j))
            pivot_rows.append([row(at[k], j) for k in range(j + 1, 8)])
            if j < 7:
                factor = jnp.where(sub > j, at[j] * inverse[j], 0.0)
                for k in range(j + 1, 8):
                    at[k] = at[k] - factor * pivot_rows[j][k - j - 1]
                lp = lp - factor * left_rows[j]
                rp = rp - factor * right_rows[j]
        right[p] = rp * lax.rsqrt(pivots)
        for q in range(p + 1, groups):
            at = [column(left[q], 8 * p + j) for j in range(8)]
            lq, rq = left[q], right[q]
            for j in range(8):
                factor = at[j] * inverse[j]
                for k in range(j + 1, 8):
                    at[k] = at[k] - factor * pivot_rows[j][k - j - 1]
                lq = lq - factor * left_rows[j]
                rq = rq - factor * right_rows[j]
            left[q], right[q] = lq, rq
    return jnp.concatenate(right, axis=0)


def latents_kernel(
    gram_low, gram_high, sketch_low, sketch_high, mix, before, activity, out, work, inverse, weights
):
    n = work.shape[0]
    mid = n // 2
    work[:mid, :] = gram_low[...]
    work[mid:, :] = gram_high[...]
    starts = range(0, n, BLOCK)
    for a in starts:
        e = a + BLOCK
        inverse[a:e, :] = inverse_factor(work[a:e, a:e])
        if e < n:
            below = product(work[e:, a:e], inverse[a:e, :], 1, 1, precise)
            work[e:, a:e] = below
            work[e:, e:] = work[e:, e:] - product(below, below, 1, 1, precise)
    for a in reversed(starts):
        e = a + BLOCK
        rest = mix[:, a:e]
        if e < n:
            rest = rest - product(weights[:, e:], work[e:, a:e], 1, 0, precise)
        weights[:, a:e] = product(rest, inverse[a:e, :], 1, 0, precise)
    loading = product(weights[:, :mid], sketch_low[...], 1, 0, precise)
    loading = loading + product(weights[:, mid:], sketch_high[...], 1, 0, precise)
    loading = loading.astype(half)
    rank = loading.shape[0]
    pieces, rows, width = out.shape
    prior = product(before[...], loading, 1, 1)
    for i in range(pieces):
        out[i, :rank, :] = product(
            loading, activity[:, i * width : (i + 1) * width], 1, 0
        )
        out[i, rank:, :] = jnp.zeros((rows - rank, width), full)
        out[i, rank:, :rank] = prior[: rows - rank, :]


def in_vmem(count):
    return [pl.BlockSpec(memory_space=pltpu.VMEM)] * count


def latent_parts(gram, sketch, mix, before, activity, pieces):
    n = mix.shape[1]
    rank = mix.shape[0]
    frames = activity.shape[1]
    return pl.pallas_call(
        latents_kernel,
        out_shape=jax.ShapeDtypeStruct((pieces, rank + 8, frames // pieces), full),
        in_specs=in_vmem(7),
        out_specs=in_vmem(1)[0],
        scratch_shapes=[
            pltpu.VMEM((n, n), full),
            pltpu.VMEM((n, BLOCK), full),
            pltpu.VMEM((rank, n), full),
        ],
        compiler_params=pltpu.CompilerParams(vmem_limit_bytes=40 * 2**20),
        cost_estimate=pl.CostEstimate(
            flops=2 * n**3, bytes_accessed=8 * 2**20, transcendentals=n
        ),
        name="latent_parts",
    )(*gram, *sketch, mix, before, activity)


def lag(block, carry):
    lane = lax.broadcasted_iota(jnp.int32, block.shape, 1)
    return jnp.where(lane == 0, carry, pltpu.roll(block, 1, 1))


def as_column(line):
    n = line.shape[1]
    square = (n, n)
    same = lax.broadcasted_iota(jnp.int32, square, 0) == lax.broadcasted_iota(jnp.int32, square, 1)
    return jnp.sum(jnp.where(same, line, 0.0), axis=1, keepdims=True)


def split(x):
    high = x.astype(half)
    return high, (x - high.astype(full)).astype(half)


def error_kernel(
    latents, signals, activity, maps, recurrent, bias,
    latents_out, frame_out, stats, cross, cross_low, squares,
):
    pieces, _, width = latents.shape
    rank = recurrent.shape[0]
    neurons = activity.shape[0]
    groups = neurons // BLOCK
    last_latent = as_column(latents[0, rank : rank + 1, :rank])
    last_signal = as_column(signals[0, rank : rank + 16, :].astype(full)[:1, :rank])
    hidden_total = jnp.zeros((rank, BLOCK), full)
    for i in range(pieces):
        frames = slice(i * width, (i + 1) * width)
        latent = latents[i, :rank, :]
        signal = signals[i, :rank, :].astype(full)
        latents_out[:, frames] = latent
        lagged_latent = lag(latent, last_latent)
        lagged_signal = lag(signal, last_signal)
        last_latent = latent[:, width - 1 :]
        last_signal = signal[:, width - 1 :]
        hidden = jnp.tanh(product(recurrent[...], lagged_latent, 1, 0, precise) + bias[...])
        high, low = split(hidden)
        state = jnp.concatenate([high, lagged_signal.astype(half)], axis=0)
        both = jnp.concatenate([high, low], axis=0)
        error = activity[:, frames].astype(full) - product(maps[...], state, 1, 0)
        error_high, error_low = split(error)
        by_both = product(error_high, both, 1, 1)
        by_high = product(error_low, high, 1, 1)
        squared = error * error
        frame_out[:, frames] = jnp.sum(squared, axis=0, keepdims=True)
        total = squared[:, :BLOCK]
        hidden_square = hidden * hidden
        for a in range(0, width, BLOCK):
            if a:
                total = total + squared[:, a : a + BLOCK]
            hidden_total = hidden_total + hidden_square[:, a : a + BLOCK]
        if i:
            cross[...] += by_both
            cross_low[...] += by_high
            squares[...] += total
        else:
            cross[...] = by_both
            cross_low[...] = by_high
            squares[...] = total
    error_sq = product(jnp.ones((8, BLOCK), full), squares[...], 1, 1, precise)
    hidden_sq = jnp.sum(hidden_total, axis=1, keepdims=True)
    stats[:, groups:, :] = jnp.zeros((rank, 2, BLOCK), full)
    for g in range(groups):
        lanes = slice(g * BLOCK, (g + 1) * BLOCK)
        by_both = cross[lanes, :].T
        by_high = cross_low[lanes, :].T
        stats[:, g, :] = by_both[:rank, :] + by_both[rank:, :] + by_high
        stats[g, groups + 1 : groups + 2, :] = error_sq[:1, lanes]
    stats[:, groups, :] = jnp.broadcast_to(hidden_sq, (rank, BLOCK))


def error_stats(latents, signals, activity, maps, recurrent, bias):
    neurons, frames = activity.shape
    rank = recurrent.shape[0]
    return pl.pallas_call(
        error_kernel,
        out_shape=(
            jax.ShapeDtypeStruct((rank, frames), full),
            jax.ShapeDtypeStruct((1, frames), full),
            jax.ShapeDtypeStruct((rank, neurons // BLOCK + 2, BLOCK), full),
        ),
        in_specs=in_vmem(6),
        out_specs=tuple(in_vmem(3)),
        scratch_shapes=[
            pltpu.VMEM((neurons, 2 * rank), full),
            pltpu.VMEM((neurons, rank), full),
            pltpu.VMEM((neurons, BLOCK), full),
        ],
        compiler_params=pltpu.CompilerParams(vmem_limit_bytes=40 * 2**20),
        cost_estimate=pl.CostEstimate(
            flops=8 * neurons * frames * rank, bytes_accessed=8 * 2**20, transcendentals=rank * frames
        ),
        name="error_stats",
    )(latents, signals, activity, maps, recurrent, bias)


def score_kernel(frames_all, stats, out):
    groups = stats.shape[1] - 2
    hidden_sq = stats[:, groups, :]
    for g in range(groups):
        lanes = slice(g * BLOCK, (g + 1) * BLOCK)
        error_sq = stats[g, groups + 1 : groups + 2, :]
        out[:, lanes] = stats[:, g, :] / jnp.sqrt(
            frames_all * (error_sq / frames_all + epsilon) * (hidden_sq / frames_all + epsilon)
        )


def scores(stats, frames_all):
    rank, rows, _ = stats.shape
    return pl.pallas_call(
        functools.partial(score_kernel, float(frames_all)),
        out_shape=jax.ShapeDtypeStruct((rank, (rows - 2) * BLOCK), full),
        in_specs=in_vmem(1),
        out_specs=in_vmem(1)[0],
        name="scores",
    )(stats)


def region_tables(block_regions, region_mask, region_in, region_out):
    regions = region_mask.shape[0]
    signal_width = region_in.shape[1]
    block_total = block_regions.shape[0]
    block_rows = region_in.shape[0] // block_total
    onehot = (block_regions[:, None] == jnp.arange(regions, dtype=jnp.int32)[None, :]).astype(full)
    onehot = jnp.broadcast_to(onehot[:, None, :], (block_total, block_rows, regions)).reshape(
        block_total * block_rows, regions
    )
    allowed = jnp.dot(onehot, region_mask.astype(full), precision=precise)
    region_feed = (onehot[:, :, None] * region_in.astype(full)[:, None, :]).reshape(
        -1, regions * signal_width
    )
    spread = (allowed[:, :, None] * region_out.astype(full)[:, None, :]).reshape(
        -1, regions * signal_width
    )
    return (region_feed.astype(half), spread.astype(half))


def local(
    activity,
    test_matrix,
    basis_mix,
    recurrent,
    latent_bias,
    readout,
    region_in,
    region_out,
    region_of_block,
    region_mask,
):
    neurons_here, frames_here = activity.shape
    columns = test_matrix.shape[1] * lax.axis_size("region")
    chips = lax.axis_size("chip")
    slabs = chips * CORES
    regions = lax.axis_size("region")
    core = lax.axis_index("core")

    test_full = lax.all_gather(test_matrix.T, "region", axis=0, tiled=True)
    before = lax.ppermute(activity[:, -1], SLAB, [(i, i + 1) for i in range(slabs - 1)])
    before = jnp.broadcast_to(before[None, :], (16, neurons_here))

    block_count = neurons_here // BLOCK
    my_blocks = lax.dynamic_slice_in_dim(
        region_of_block, lax.axis_index("region") * block_count, block_count
    )
    region_feed, spread = region_tables(my_blocks, region_mask, region_in, region_out)
    maps = jnp.concatenate([readout, spread], axis=1)
    rank = region_feed.shape[1]
    signal = product(region_feed, activity, 0, 0)
    signal = signal.reshape(rank, regions, -1).transpose(1, 0, 2)
    prior = product(before, region_feed, 1, 0)
    prior = jnp.pad(prior, ((0, 0), (0, signal.shape[2] - rank)))
    prior = jnp.broadcast_to(prior[None], (regions,) + prior.shape)
    signal = scatter_sum(jnp.concatenate([signal, prior], axis=1), "region")
    signals = share(signal.astype(half), "region")
    bias = latent_bias[:, None]
    test_full, signals, maps, before, bias = lax.optimization_barrier(
        (test_full, signals, maps, before, bias)
    )

    mid = columns // CORES
    theirs = product(lax.dynamic_slice_in_dim(test_full, (1 - core) * mid, mid), activity, 1, 1)
    mine = product(lax.dynamic_slice_in_dim(test_full, core * mid, mid), activity, 1, 1)
    mine = mine + other_core(theirs)
    own = scatter_sum(mine.reshape(chips, mid // chips, neurons_here), "chip")
    mine = share(own, "chip").reshape(mid, neurons_here)
    sketch = in_core_order(mine, other_core(mine))

    rows = jnp.concatenate([product(own, part, 1, 1, precise) for part in sketch], axis=1)
    rows = jnp.sum(share(rows, "region"), axis=0)
    mine = share(rows, "chip").reshape(mid, columns)
    gram = in_core_order(mine, other_core(mine))

    parts = latent_parts(gram, sketch, basis_mix.T, before, activity, regions)
    latents = share(scatter_sum(parts, "region"), "region")
    latents_out, frame_sq, stats = error_stats(
        latents, signals, activity, maps, recurrent, bias
    )
    frame_sq = lax.psum(frame_sq.reshape(frames_here), "region")
    stats = stats.reshape((slabs, rank // slabs) + stats.shape[1:])
    stats = share(scatter_sum(stats, SLAB), SLAB)
    stats = stats.reshape((rank,) + stats.shape[2:])
    score = scores(stats, frames_here * slabs)
    return (latents_out, frame_sq / (neurons_here * regions), score.T)


def solution(mesh):
    slabs, regions = mesh.devices.shape
    devices = mesh.devices.reshape(slabs // CORES, CORES, regions)
    mesh = Mesh(devices, ("chip", "core", "region"))
    in_specs = (
        P("region", SLAB),
        P(SLAB, "region"),
        P(),
        P(),
        P(),
        P("region", None),
        P("region", None),
        P("region", None),
        P(),
        P(),
    )
    out_specs = (P(None, SLAB), P(SLAB), P("region", None))
    return jax.shard_map(local, mesh=mesh, in_specs=in_specs, out_specs=out_specs, check_vma=False)
```

```python
import functools

import jax
import jax.numpy as jnp
from jax import lax
from jax.experimental import pallas as pl
from jax.experimental.pallas import tpu as pltpu
from jax.sharding import Mesh
from jax.sharding import PartitionSpec as P

BLOCK = 128
CORES = 2
SLAB = ("chip", "core")

precise = lax.Precision.HIGHEST
epsilon = 1e-05
full = jnp.float32
half = jnp.bfloat16


def product(a, b, ca, cb, precision=None):
    return lax.dot_general(
        a, b, (((ca,), (cb,)), ((), ())), precision=precision, preferred_element_type=full
    )


def other_core(x):
    return lax.ppermute(x, "core", [(0, 1), (1, 0)])


def scatter_sum(pieces, axis):
    return jnp.sum(lax.all_to_all(pieces, axis, 0, 0).astype(full), axis=0)


def share(x, axis):
    copies = jnp.broadcast_to(x[None], (lax.axis_size(axis),) + x.shape)
    return lax.all_to_all(lax.optimization_barrier(copies), axis, 0, 0)


def inverse_factor(tile):
    n = tile.shape[0]
    groups = n // 8
    sub = lax.broadcasted_iota(jnp.int32, (8, n), 0)
    lane = lax.broadcasted_iota(jnp.int32, (8, n), 1)

    def column(x, j):
        return jnp.broadcast_to(x[:, j : j + 1], x.shape)

    def row(x, j):
        return jnp.broadcast_to(x[j : j + 1, :], x.shape)

    left = [tile[8 * q : 8 * q + 8, :] for q in range(groups)]
    right = [jnp.where(lane == sub + 8 * q, full(1), full(0)) for q in range(groups)]
    for p in range(groups):
        at = [column(left[p], 8 * p + j) for j in range(8)]
        lp, rp = left[p], right[p]
        pivots = jnp.ones_like(lp)
        inverse, left_rows, right_rows, pivot_rows = [], [], [], []
        for j in range(8):
            pivot = row(at[j], j)
            pivots = jnp.where(sub == j, pivot, pivots)
            inverse.append(1.0 / pivot)
            left_rows.append(row(lp, j))
            right_rows.append(row(rp, j))
            pivot_rows.append([row(at[k], j) for k in range(j + 1, 8)])
            if j < 7:
                factor = jnp.where(sub > j, at[j] * inverse[j], 0.0)
                for k in range(j + 1, 8):
                    at[k] = at[k] - factor * pivot_rows[j][k - j - 1]
                lp = lp - factor * left_rows[j]
                rp = rp - factor * right_rows[j]
        right[p] = rp * lax.rsqrt(pivots)
        for q in range(p + 1, groups):
            at = [column(left[q], 8 * p + j) for j in range(8)]
            lq, rq = left[q], right[q]
            for j in range(8):
                factor = at[j] * inverse[j]
                for k in range(j + 1, 8):
                    at[k] = at[k] - factor * pivot_rows[j][k - j - 1]
                lq = lq - factor * left_rows[j]
                rq = rq - factor * right_rows[j]
            left[q], right[q] = lq, rq
    return jnp.concatenate(right, axis=0)


def latents_kernel(
    core, gram, gram_other, sketch, sketch_other, mix, before, activity,
    out, work, inverse, weights,
):
    n = work.shape[0]
    mid = n // 2
    here = pl.ds(pl.multiple_of(core[0] * mid, mid), mid)
    there = pl.ds(pl.multiple_of((1 - core[0]) * mid, mid), mid)
    work[here, :] = gram[...]
    work[there, :] = gram_other[...]
    starts = range(0, n, BLOCK)
    for a in starts:
        e = a + BLOCK
        inverse[a:e, :] = inverse_factor(work[a:e, a:e])
        if e < n:
            below = product(work[e:, a:e], inverse[a:e, :], 1, 1, precise)
            work[e:, a:e] = below
            work[e:, e:] = work[e:, e:] - product(below, below, 1, 1, precise)
    for a in reversed(starts):
        e = a + BLOCK
        rest = mix[:, a:e]
        if e < n:
            rest = rest - product(weights[:, e:], work[e:, a:e], 1, 0, precise)
        weights[:, a:e] = product(rest, inverse[a:e, :], 1, 0, precise)
    loading = product(weights[:, here], sketch[...], 1, 0, precise)
    loading = loading + product(weights[:, there], sketch_other[...], 1, 0, precise)
    loading = loading.astype(half)
    rank = loading.shape[0]
    pieces, rows, width = out.shape
    prior = product(before[...], loading, 1, 1)
    for i in range(pieces):
        out[i, :rank, :] = product(
            loading, activity[:, i * width : (i + 1) * width], 1, 0
        )
        out[i, rank:, :] = jnp.zeros((rows - rank, width), full)
        out[i, rank:, :rank] = prior[: rows - rank, :]


def in_vmem(count):
    return [pl.BlockSpec(memory_space=pltpu.VMEM)] * count


def scalar():
    return pl.BlockSpec(memory_space=pltpu.SMEM)


def gram_kernel(core, own, sketch, sketch_other, out):
    mid = sketch.shape[0]
    mine = product(own[...], sketch[...], 1, 1, precise)
    other = product(own[...], sketch_other[...], 1, 1, precise)
    first = core[0] == 0
    low, high = jnp.where(first, mine, other), jnp.where(first, other, mine)
    for i in range(out.shape[0]):
        out[i, :, :mid] = low
        out[i, :, mid:] = high


def gram_rows(core, own, sketch, copies):
    rows, columns = own.shape[0], 2 * sketch[0].shape[0]
    return pl.pallas_call(
        gram_kernel,
        out_shape=jax.ShapeDtypeStruct((copies, rows, columns), full),
        in_specs=[scalar()] + in_vmem(3),
        out_specs=in_vmem(1)[0],
        compiler_params=pltpu.CompilerParams(vmem_limit_bytes=16 * 2**20),
        cost_estimate=pl.CostEstimate(
            flops=2 * rows * columns * own.shape[1], bytes_accessed=2 * 2**20, transcendentals=0
        ),
        name="gram_rows",
    )(core, own, *sketch)


def signals_kernel(feed, before, activity, out):
    pieces, rows, width = out.shape
    rank = feed.shape[0]
    prior = product(before[...], feed[...], 1, 1).astype(half)
    for i in range(pieces):
        signal = product(feed[...], activity[:, i * width : (i + 1) * width], 1, 0)
        out[i, :rank, :] = signal.astype(half)
        out[i, rank:, :] = jnp.zeros((rows - rank, width), half)
        out[i, rank:, :rank] = prior


def signal_parts(feed, before, activity, pieces):
    rank, neurons = feed.shape
    frames = activity.shape[1]
    return pl.pallas_call(
        signals_kernel,
        out_shape=jax.ShapeDtypeStruct((pieces, rank + before.shape[0], frames // pieces), half),
        in_specs=in_vmem(3),
        out_specs=in_vmem(1)[0],
        compiler_params=pltpu.CompilerParams(vmem_limit_bytes=16 * 2**20),
        cost_estimate=pl.CostEstimate(
            flops=2 * rank * neurons * frames, bytes_accessed=4 * 2**20, transcendentals=0
        ),
        name="signal_parts",
    )(feed, before, activity)


def latent_parts(core, gram, sketch, mix, before, activity, pieces):
    n = mix.shape[1]
    rank = mix.shape[0]
    frames = activity.shape[1]
    return pl.pallas_call(
        latents_kernel,
        out_shape=jax.ShapeDtypeStruct((pieces, rank + 8, frames // pieces), full),
        in_specs=[scalar()] + in_vmem(7),
        out_specs=in_vmem(1)[0],
        scratch_shapes=[
            pltpu.VMEM((n, n), full),
            pltpu.VMEM((n, BLOCK), full),
            pltpu.VMEM((rank, n), full),
        ],
        compiler_params=pltpu.CompilerParams(vmem_limit_bytes=40 * 2**20),
        cost_estimate=pl.CostEstimate(
            flops=2 * n**3, bytes_accessed=8 * 2**20, transcendentals=n
        ),
        name="latent_parts",
    )(core, *gram, *sketch, mix, before, activity)


def lag(block, carry):
    lane = lax.broadcasted_iota(jnp.int32, block.shape, 1)
    return jnp.where(lane == 0, carry, pltpu.roll(block, 1, 1))


def as_column(line):
    n = line.shape[1]
    square = (n, n)
    same = lax.broadcasted_iota(jnp.int32, square, 0) == lax.broadcasted_iota(jnp.int32, square, 1)
    return jnp.sum(jnp.where(same, line, 0.0), axis=1, keepdims=True)


def split(x):
    high = x.astype(half)
    return high, (x - high.astype(full)).astype(half)


def error_kernel(
    latents, signals, activity, maps, recurrent, bias,
    latents_out, frame_out, stats, cross, cross_low, squares,
):
    pieces, _, width = latents.shape
    rank = recurrent.shape[0]
    neurons = activity.shape[0]
    groups = neurons // BLOCK
    last_latent = as_column(latents[0, rank : rank + 1, :rank])
    last_signal = as_column(signals[0, rank : rank + 16, :].astype(full)[:1, :rank])
    hidden_total = jnp.zeros((rank, BLOCK), full)
    for i in range(pieces):
        frames = slice(i * width, (i + 1) * width)
        latent = latents[i, :rank, :]
        signal = signals[i, :rank, :].astype(full)
        latents_out[:, frames] = latent
        lagged_latent = lag(latent, last_latent)
        lagged_signal = lag(signal, last_signal)
        last_latent = latent[:, width - 1 :]
        last_signal = signal[:, width - 1 :]
        hidden = jnp.tanh(product(recurrent[...], lagged_latent, 1, 0, precise) + bias[...])
        high, low = split(hidden)
        state = jnp.concatenate([high, lagged_signal.astype(half)], axis=0)
        both = jnp.concatenate([high, low], axis=0)
        error = activity[:, frames].astype(full) - product(maps[...], state, 1, 0)
        error_high, error_low = split(error)
        by_both = product(error_high, both, 1, 1)
        by_high = product(error_low, high, 1, 1)
        squared = error * error
        frame_out[:, frames] = jnp.sum(squared, axis=0, keepdims=True)
        total = squared[:, :BLOCK]
        hidden_square = hidden * hidden
        for a in range(0, width, BLOCK):
            if a:
                total = total + squared[:, a : a + BLOCK]
            hidden_total = hidden_total + hidden_square[:, a : a + BLOCK]
        if i:
            cross[...] += by_both
            cross_low[...] += by_high
            squares[...] += total
        else:
            cross[...] = by_both
            cross_low[...] = by_high
            squares[...] = total
    error_sq = product(jnp.ones((8, BLOCK), full), squares[...], 1, 1, precise)
    hidden_sq = jnp.sum(hidden_total, axis=1, keepdims=True)
    stats[:, groups:, :] = jnp.zeros((rank, 2, BLOCK), full)
    for g in range(groups):
        lanes = slice(g * BLOCK, (g + 1) * BLOCK)
        by_both = cross[lanes, :].T
        by_high = cross_low[lanes, :].T
        stats[:, g, :] = by_both[:rank, :] + by_both[rank:, :] + by_high
        stats[g, groups + 1 : groups + 2, :] = error_sq[:1, lanes]
    stats[:, groups, :] = jnp.broadcast_to(hidden_sq, (rank, BLOCK))


def error_stats(latents, signals, activity, maps, recurrent, bias):
    neurons, frames = activity.shape
    rank = recurrent.shape[0]
    return pl.pallas_call(
        error_kernel,
        out_shape=(
            jax.ShapeDtypeStruct((rank, frames), full),
            jax.ShapeDtypeStruct((1, frames), full),
            jax.ShapeDtypeStruct((rank, neurons // BLOCK + 2, BLOCK), full),
        ),
        in_specs=in_vmem(6),
        out_specs=tuple(in_vmem(3)),
        scratch_shapes=[
            pltpu.VMEM((neurons, 2 * rank), full),
            pltpu.VMEM((neurons, rank), full),
            pltpu.VMEM((neurons, BLOCK), full),
        ],
        compiler_params=pltpu.CompilerParams(vmem_limit_bytes=40 * 2**20),
        cost_estimate=pl.CostEstimate(
            flops=8 * neurons * frames * rank, bytes_accessed=8 * 2**20, transcendentals=rank * frames
        ),
        name="error_stats",
    )(latents, signals, activity, maps, recurrent, bias)


def score_kernel(frames_all, stats, out):
    groups = stats.shape[1] - 2
    hidden_sq = stats[:, groups, :]
    for g in range(groups):
        lanes = slice(g * BLOCK, (g + 1) * BLOCK)
        error_sq = stats[g, groups + 1 : groups + 2, :]
        out[:, lanes] = stats[:, g, :] / jnp.sqrt(
            frames_all * (error_sq / frames_all + epsilon) * (hidden_sq / frames_all + epsilon)
        )


def scores(stats, frames_all):
    rank, rows, _ = stats.shape
    return pl.pallas_call(
        functools.partial(score_kernel, float(frames_all)),
        out_shape=jax.ShapeDtypeStruct((rank, (rows - 2) * BLOCK), full),
        in_specs=in_vmem(1),
        out_specs=in_vmem(1)[0],
        name="scores",
    )(stats)


def region_tables(block_regions, region_mask, region_in, region_out):
    regions = region_mask.shape[0]
    signal_width = region_in.shape[1]
    block_total = block_regions.shape[0]
    block_rows = region_in.shape[0] // block_total
    onehot = (block_regions[:, None] == jnp.arange(regions, dtype=jnp.int32)[None, :]).astype(full)
    onehot = jnp.broadcast_to(onehot[:, None, :], (block_total, block_rows, regions)).reshape(
        block_total * block_rows, regions
    )
    allowed = jnp.dot(onehot, region_mask.astype(full), precision=precise)
    region_feed = (onehot[:, :, None] * region_in.astype(full)[:, None, :]).reshape(
        -1, regions * signal_width
    )
    spread = (allowed[:, :, None] * region_out.astype(full)[:, None, :]).reshape(
        -1, regions * signal_width
    )
    return (region_feed.astype(half), spread.astype(half))


def local(
    activity,
    test_matrix,
    basis_mix,
    recurrent,
    latent_bias,
    readout,
    region_in,
    region_out,
    region_of_block,
    region_mask,
):
    neurons_here, frames_here = activity.shape
    columns = test_matrix.shape[1] * lax.axis_size("region")
    chips = lax.axis_size("chip")
    slabs = chips * CORES
    regions = lax.axis_size("region")
    core = lax.axis_index("core")

    test_full = lax.all_gather(test_matrix.T, "region", axis=0, tiled=True)
    before = lax.ppermute(activity[:, -1], SLAB, [(i, i + 1) for i in range(slabs - 1)])
    before = jnp.broadcast_to(before[None, :], (16, neurons_here))

    block_count = neurons_here // BLOCK
    my_blocks = lax.dynamic_slice_in_dim(
        region_of_block, lax.axis_index("region") * block_count, block_count
    )
    region_feed, spread = region_tables(my_blocks, region_mask, region_in, region_out)
    maps = jnp.concatenate([readout, spread], axis=1)
    rank = region_feed.shape[1]
    signal = signal_parts(region_feed.T, before, activity, regions)
    signals = share(scatter_sum(signal, "region").astype(half), "region")

    largest = jnp.maximum(jnp.max(jnp.abs(basis_mix), axis=0), 1e-30)
    width = frames_here // regions
    unit = jnp.concatenate(
        [
            jnp.broadcast_to(largest[:, None], (rank, width)),
            jnp.broadcast_to(jnp.pad(largest, (0, width - rank), constant_values=1.0), (8, width)),
        ]
    )
    unit = unit / 4
    bias = latent_bias[:, None]
    test_full, signals, maps, before, bias, unit, per_unit = lax.optimization_barrier(
        (test_full, signals, maps, before, bias, unit, 1 / unit)
    )

    mid = columns // CORES
    theirs = product(lax.dynamic_slice_in_dim(test_full, (1 - core) * mid, mid), activity, 1, 1)
    theirs = other_core(theirs)
    mine = product(lax.dynamic_slice_in_dim(test_full, core * mid, mid), activity, 1, 1)
    mine = lax.optimization_barrier(mine) + theirs
    own = scatter_sum(mine.reshape(chips, mid // chips, neurons_here), "chip")
    mine = share(own, "chip").reshape(mid, neurons_here)
    sketch = mine, other_core(mine)

    core = core.reshape(1)
    rows = lax.all_to_all(gram_rows(core, own, sketch, regions), "region", 0, 0)
    rows = jnp.sum(rows, axis=0)
    mine = share(rows, "chip").reshape(mid, columns)
    gram = mine, other_core(mine)

    parts = latent_parts(core, gram, sketch, basis_mix.T, before, activity, regions)
    latents = scatter_sum((parts * per_unit).astype(jnp.float16), "region")
    latents = share(latents.astype(jnp.float16), "region").astype(full) * unit
    latents_out, frame_sq, stats = error_stats(
        latents, signals, activity, maps, recurrent, bias
    )
    frame_sq = lax.psum(frame_sq.reshape(frames_here), "region")
    stats = stats.reshape((slabs, rank // slabs) + stats.shape[1:])
    stats = share(scatter_sum(stats, SLAB), SLAB)
    stats = stats.reshape((rank,) + stats.shape[2:])
    score = scores(stats, frames_here * slabs)
    return (latents_out, frame_sq / (neurons_here * regions), score.T)


def solution(mesh):
    slabs, regions = mesh.devices.shape
    devices = mesh.devices.reshape(slabs // CORES, CORES, regions)
    mesh = Mesh(devices, ("chip", "core", "region"))
    in_specs = (
        P("region", SLAB),
        P(SLAB, "region"),
        P(),
        P(),
        P(),
        P("region", None),
        P("region", None),
        P("region", None),
        P(),
        P(),
    )
    out_specs = (P(None, SLAB), P(SLAB), P("region", None))
    return jax.shard_map(local, mesh=mesh, in_specs=in_specs, out_specs=out_specs, check_vma=False)
```

```python
import functools

import jax
import jax.numpy as jnp
from jax import lax
from jax.experimental import pallas as pl
from jax.experimental.pallas import tpu as pltpu
from jax.sharding import Mesh
from jax.sharding import PartitionSpec as P

BLOCK = 128
CORES = 2
SLAB = ("chip", "core")

precise = lax.Precision.HIGHEST
epsilon = 1e-05
full = jnp.float32
half = jnp.bfloat16


def product(a, b, ca, cb, precision=None):
    return lax.dot_general(
        a, b, (((ca,), (cb,)), ((), ())), precision=precision, preferred_element_type=full
    )


def other_core(x):
    return lax.ppermute(x, "core", [(0, 1), (1, 0)])


def scatter_sum(pieces, axis):
    return jnp.sum(lax.all_to_all(pieces, axis, 0, 0).astype(full), axis=0)


def share(x, axis):
    copies = jnp.broadcast_to(x[None], (lax.axis_size(axis),) + x.shape)
    return lax.all_to_all(lax.optimization_barrier(copies), axis, 0, 0)


def inverse_factor(tile):
    n = tile.shape[0]
    groups = n // 8
    sub = lax.broadcasted_iota(jnp.int32, (8, n), 0)
    lane = lax.broadcasted_iota(jnp.int32, (8, n), 1)

    def column(x, j):
        return jnp.broadcast_to(x[:, j : j + 1], x.shape)

    def row(x, j):
        return jnp.broadcast_to(x[j : j + 1, :], x.shape)

    left = [tile[8 * q : 8 * q + 8, :] for q in range(groups)]
    right = [jnp.where(lane == sub + 8 * q, full(1), full(0)) for q in range(groups)]
    for p in range(groups):
        at = [column(left[p], 8 * p + j) for j in range(8)]
        lp, rp = left[p], right[p]
        pivots = jnp.ones_like(lp)
        inverse, left_rows, right_rows, pivot_rows = [], [], [], []
        for j in range(8):
            pivot = row(at[j], j)
            pivots = jnp.where(sub == j, pivot, pivots)
            inverse.append(1.0 / pivot)
            left_rows.append(row(lp, j))
            right_rows.append(row(rp, j))
            pivot_rows.append([row(at[k], j) for k in range(j + 1, 8)])
            if j < 7:
                factor = jnp.where(sub > j, at[j] * inverse[j], 0.0)
                for k in range(j + 1, 8):
                    at[k] = at[k] - factor * pivot_rows[j][k - j - 1]
                lp = lp - factor * left_rows[j]
                rp = rp - factor * right_rows[j]
        right[p] = rp * lax.rsqrt(pivots)
        for q in range(p + 1, groups):
            at = [column(left[q], 8 * p + j) for j in range(8)]
            lq, rq = left[q], right[q]
            for j in range(8):
                factor = at[j] * inverse[j]
                for k in range(j + 1, 8):
                    at[k] = at[k] - factor * pivot_rows[j][k - j - 1]
                lq = lq - factor * left_rows[j]
                rq = rq - factor * right_rows[j]
            left[q], right[q] = lq, rq
    return jnp.concatenate(right, axis=0)


def fetch(sources, targets, arrived):
    copies = [
        pltpu.make_async_copy(source, target, arrived.at[i])
        for i, (source, target) in enumerate(zip(sources, targets))
    ]
    for copy in copies:
        copy.start()
    return copies


def latents_kernel(
    core, gram, gram_other, before, sketch, sketch_other, mix, activity,
    out, work, inverse, weights, sketch_here, mix_here, activity_here, arrived,
):
    copies = fetch(
        (sketch, sketch_other, mix, activity),
        (sketch_here.at[0], sketch_here.at[1], mix_here, activity_here),
        arrived,
    )
    n = work.shape[0]
    mid = n // 2
    here = pl.ds(pl.multiple_of(core[0] * mid, mid), mid)
    there = pl.ds(pl.multiple_of((1 - core[0]) * mid, mid), mid)
    work[here, :] = gram[...]
    work[there, :] = gram_other[...]
    starts = range(0, n, BLOCK)
    diagonal = work[:BLOCK, :BLOCK]
    for a in starts:
        e = a + BLOCK
        factor = inverse_factor(diagonal)
        inverse[a:e, :] = factor
        if e < n:
            z = e + BLOCK
            near = product(work[e:z, a:e], factor, 1, 1, precise)
            diagonal = work[e:z, e:z] - product(near, near, 1, 1, precise)
            work[e:z, a:e] = near
        if e < n and z < n:
            far = product(work[z:, a:e], factor, 1, 1, precise)
            work[z:, a:e] = far
            work[z:, e:z] = work[z:, e:z] - product(far, near, 1, 1, precise)
            work[z:, z:] = work[z:, z:] - product(far, far, 1, 1, precise)
    copies[2].wait()
    for a in reversed(starts):
        e = a + BLOCK
        rest = mix_here[:, a:e]
        if e < n:
            rest = rest - product(weights[:, e:], work[e:, a:e], 1, 0, precise)
        weights[:, a:e] = product(rest, inverse[a:e, :], 1, 0, precise)
    copies[0].wait()
    copies[1].wait()
    loading = product(weights[:, here], sketch_here[0], 1, 0, precise)
    loading = loading + product(weights[:, there], sketch_here[1], 1, 0, precise)
    loading = loading.astype(half)
    rank = loading.shape[0]
    pieces, rows, width = out.shape
    prior = product(before[...], loading, 1, 1)
    copies[3].wait()
    for i in range(pieces):
        out[i, :rank, :] = product(
            loading, activity_here[:, i * width : (i + 1) * width], 1, 0
        )
        out[i, rank:, :] = jnp.zeros((rows - rank, width), full)
        out[i, rank:, :rank] = prior[: rows - rank, :]


def in_vmem(count):
    return [pl.BlockSpec(memory_space=pltpu.VMEM)] * count


def anywhere(count):
    return [pl.BlockSpec(memory_space=pl.ANY)] * count


def scalar():
    return pl.BlockSpec(memory_space=pltpu.SMEM)


def gram_kernel(core, own, sketch, sketch_other, out):
    mid = sketch.shape[0]
    mine = product(own[...], sketch[...], 1, 1, precise)
    other = product(own[...], sketch_other[...], 1, 1, precise)
    first = core[0] == 0
    low, high = jnp.where(first, mine, other), jnp.where(first, other, mine)
    for i in range(out.shape[0]):
        out[i, :, :mid] = low
        out[i, :, mid:] = high


def gram_rows(core, own, sketch, copies):
    rows, columns = own.shape[0], 2 * sketch[0].shape[0]
    return pl.pallas_call(
        gram_kernel,
        out_shape=jax.ShapeDtypeStruct((copies, rows, columns), full),
        in_specs=[scalar()] + in_vmem(3),
        out_specs=in_vmem(1)[0],
        compiler_params=pltpu.CompilerParams(vmem_limit_bytes=16 * 2**20),
        cost_estimate=pl.CostEstimate(
            flops=2 * rows * columns * own.shape[1], bytes_accessed=2 * 2**20, transcendentals=0
        ),
        name="gram_rows",
    )(core, own, *sketch)


def signals_kernel(feed, before, activity, out):
    pieces, rows, width = out.shape
    rank = feed.shape[0]
    prior = product(before[...], feed[...], 1, 1).astype(half)
    for i in range(pieces):
        signal = product(feed[...], activity[:, i * width : (i + 1) * width], 1, 0)
        out[i, :rank, :] = signal.astype(half)
        out[i, rank:, :] = jnp.zeros((rows - rank, width), half)
        out[i, rank:, :rank] = prior


def signal_parts(feed, before, activity, pieces):
    rank, neurons = feed.shape
    frames = activity.shape[1]
    return pl.pallas_call(
        signals_kernel,
        out_shape=jax.ShapeDtypeStruct((pieces, rank + before.shape[0], frames // pieces), half),
        in_specs=in_vmem(3),
        out_specs=in_vmem(1)[0],
        compiler_params=pltpu.CompilerParams(vmem_limit_bytes=16 * 2**20),
        cost_estimate=pl.CostEstimate(
            flops=2 * rank * neurons * frames, bytes_accessed=4 * 2**20, transcendentals=0
        ),
        name="signal_parts",
    )(feed, before, activity)


def latent_parts(core, gram, sketch, mix, before, activity, pieces):
    n = mix.shape[1]
    rank = mix.shape[0]
    frames = activity.shape[1]
    return pl.pallas_call(
        latents_kernel,
        out_shape=jax.ShapeDtypeStruct((pieces, rank + 8, frames // pieces), full),
        in_specs=[scalar()] + in_vmem(3) + anywhere(4),
        out_specs=in_vmem(1)[0],
        scratch_shapes=[
            pltpu.VMEM((n, n), full),
            pltpu.VMEM((n, BLOCK), full),
            pltpu.VMEM((rank, n), full),
            pltpu.VMEM((2,) + sketch[0].shape, full),
            pltpu.VMEM((rank, n), full),
            pltpu.VMEM(activity.shape, half),
            pltpu.SemaphoreType.DMA((4,)),
        ],
        compiler_params=pltpu.CompilerParams(vmem_limit_bytes=58 * 2**20),
        cost_estimate=pl.CostEstimate(
            flops=2 * n**3, bytes_accessed=8 * 2**20, transcendentals=n
        ),
        name="latent_parts",
    )(core, *gram, before, *sketch, mix, activity)


def lag(block, carry):
    lane = lax.broadcasted_iota(jnp.int32, block.shape, 1)
    return jnp.where(lane == 0, carry, pltpu.roll(block, 1, 1))


def as_column(line):
    n = line.shape[1]
    square = (n, n)
    same = lax.broadcasted_iota(jnp.int32, square, 0) == lax.broadcasted_iota(jnp.int32, square, 1)
    return jnp.sum(jnp.where(same, line, 0.0), axis=1, keepdims=True)


def split(x):
    high = x.astype(half)
    return high, (x - high.astype(full)).astype(half)


def error_kernel(
    latents, signals, activity, maps, recurrent, bias,
    latents_out, frame_out, stats, cross, cross_low, squares, maps_here, arrived,
):
    copies = fetch((maps,), (maps_here,), arrived)
    pieces, _, width = latents.shape
    rank = recurrent.shape[0]
    neurons = activity.shape[0]
    groups = neurons // BLOCK
    last_latent = as_column(latents[0, rank : rank + 1, :rank])
    last_signal = as_column(signals[0, rank : rank + 16, :].astype(full)[:1, :rank])
    hidden_total = jnp.zeros((rank, BLOCK), full)
    for i in range(pieces):
        frames = slice(i * width, (i + 1) * width)
        latent = latents[i, :rank, :]
        signal = signals[i, :rank, :].astype(full)
        latents_out[:, frames] = latent
        lagged_latent = lag(latent, last_latent)
        lagged_signal = lag(signal, last_signal)
        last_latent = latent[:, width - 1 :]
        last_signal = signal[:, width - 1 :]
        hidden = jnp.tanh(product(recurrent[...], lagged_latent, 1, 0, precise) + bias[...])
        high, low = split(hidden)
        state = jnp.concatenate([high, lagged_signal.astype(half)], axis=0)
        both = jnp.concatenate([high, low], axis=0)
        if not i:
            copies[0].wait()
        error = activity[:, frames].astype(full) - product(maps_here[...], state, 1, 0)
        error_high, error_low = split(error)
        by_both = product(error_high, both, 1, 1)
        by_high = product(error_low, high, 1, 1)
        squared = error * error
        frame_out[:, frames] = jnp.sum(squared, axis=0, keepdims=True)
        total = squared[:, :BLOCK]
        hidden_square = hidden * hidden
        for a in range(0, width, BLOCK):
            if a:
                total = total + squared[:, a : a + BLOCK]
            hidden_total = hidden_total + hidden_square[:, a : a + BLOCK]
        if i:
            cross[...] += by_both
            cross_low[...] += by_high
            squares[...] += total
        else:
            cross[...] = by_both
            cross_low[...] = by_high
            squares[...] = total
    error_sq = product(jnp.ones((8, BLOCK), full), squares[...], 1, 1, precise)
    hidden_sq = jnp.sum(hidden_total, axis=1, keepdims=True)
    stats[:, groups:, :] = jnp.zeros((rank, 2, BLOCK), full)
    for g in range(groups):
        lanes = slice(g * BLOCK, (g + 1) * BLOCK)
        by_both = cross[lanes, :].T
        by_high = cross_low[lanes, :].T
        stats[:, g, :] = by_both[:rank, :] + by_both[rank:, :] + by_high
        stats[g, groups + 1 : groups + 2, :] = error_sq[:1, lanes]
    stats[:, groups, :] = jnp.broadcast_to(hidden_sq, (rank, BLOCK))


def error_stats(latents, signals, activity, maps, recurrent, bias):
    neurons, frames = activity.shape
    rank = recurrent.shape[0]
    return pl.pallas_call(
        error_kernel,
        out_shape=(
            jax.ShapeDtypeStruct((rank, frames), full),
            jax.ShapeDtypeStruct((1, frames), full),
            jax.ShapeDtypeStruct((rank, neurons // BLOCK + 2, BLOCK), full),
        ),
        in_specs=in_vmem(3) + anywhere(1) + in_vmem(2),
        out_specs=tuple(in_vmem(3)),
        scratch_shapes=[
            pltpu.VMEM((neurons, 2 * rank), full),
            pltpu.VMEM((neurons, rank), full),
            pltpu.VMEM((neurons, BLOCK), full),
            pltpu.VMEM(maps.shape, half),
            pltpu.SemaphoreType.DMA((1,)),
        ],
        compiler_params=pltpu.CompilerParams(vmem_limit_bytes=40 * 2**20),
        cost_estimate=pl.CostEstimate(
            flops=8 * neurons * frames * rank, bytes_accessed=8 * 2**20, transcendentals=rank * frames
        ),
        name="error_stats",
    )(latents, signals, activity, maps, recurrent, bias)


def score_kernel(frames_all, stats, out):
    groups = stats.shape[1] - 2
    hidden_sq = stats[:, groups, :]
    for g in range(groups):
        lanes = slice(g * BLOCK, (g + 1) * BLOCK)
        error_sq = stats[g, groups + 1 : groups + 2, :]
        out[:, lanes] = stats[:, g, :] / jnp.sqrt(
            frames_all * (error_sq / frames_all + epsilon) * (hidden_sq / frames_all + epsilon)
        )


def scores(stats, frames_all):
    rank, rows, _ = stats.shape
    return pl.pallas_call(
        functools.partial(score_kernel, float(frames_all)),
        out_shape=jax.ShapeDtypeStruct((rank, (rows - 2) * BLOCK), full),
        in_specs=in_vmem(1),
        out_specs=in_vmem(1)[0],
        name="scores",
    )(stats)


def region_tables(block_regions, region_mask, region_in, region_out):
    regions = region_mask.shape[0]
    signal_width = region_in.shape[1]
    block_total = block_regions.shape[0]
    block_rows = region_in.shape[0] // block_total
    onehot = (block_regions[:, None] == jnp.arange(regions, dtype=jnp.int32)[None, :]).astype(full)
    onehot = jnp.broadcast_to(onehot[:, None, :], (block_total, block_rows, regions)).reshape(
        block_total * block_rows, regions
    )
    allowed = jnp.dot(onehot, region_mask.astype(full), precision=precise)
    region_feed = (onehot[:, :, None] * region_in.astype(full)[:, None, :]).reshape(
        -1, regions * signal_width
    )
    spread = (allowed[:, :, None] * region_out.astype(full)[:, None, :]).reshape(
        -1, regions * signal_width
    )
    return (region_feed.astype(half), spread.astype(half))


def local(
    activity,
    test_matrix,
    basis_mix,
    recurrent,
    latent_bias,
    readout,
    region_in,
    region_out,
    region_of_block,
    region_mask,
):
    neurons_here, frames_here = activity.shape
    columns = test_matrix.shape[1] * lax.axis_size("region")
    chips = lax.axis_size("chip")
    slabs = chips * CORES
    regions = lax.axis_size("region")
    core = lax.axis_index("core")

    test_full = lax.all_gather(test_matrix.T, "region", axis=0, tiled=True)
    before = lax.ppermute(activity[:, -1], SLAB, [(i, i + 1) for i in range(slabs - 1)])
    before = jnp.broadcast_to(before[None, :], (16, neurons_here))

    block_count = neurons_here // BLOCK
    my_blocks = lax.dynamic_slice_in_dim(
        region_of_block, lax.axis_index("region") * block_count, block_count
    )
    region_feed, spread = region_tables(my_blocks, region_mask, region_in, region_out)
    maps = jnp.concatenate([readout, spread], axis=1)
    rank = region_feed.shape[1]
    signal = signal_parts(region_feed.T, before, activity, regions)
    signal = scatter_sum(signal, "region").astype(half)

    largest = jnp.maximum(jnp.max(jnp.abs(basis_mix), axis=0), 1e-30)
    width = frames_here // regions
    unit = jnp.concatenate(
        [
            jnp.broadcast_to(largest[:, None], (rank, width)),
            jnp.broadcast_to(jnp.pad(largest, (0, width - rank), constant_values=1.0), (8, width)),
        ]
    )
    unit = unit / 4
    bias = latent_bias[:, None]
    test_full, signal, maps, before, bias, unit, per_unit = lax.optimization_barrier(
        (test_full, signal, maps, before, bias, unit, 1 / unit)
    )

    mid = columns // CORES
    theirs = product(lax.dynamic_slice_in_dim(test_full, (1 - core) * mid, mid), activity, 1, 1)
    theirs = other_core(theirs)
    mine = product(lax.dynamic_slice_in_dim(test_full, core * mid, mid), activity, 1, 1)
    mine = lax.optimization_barrier(mine) + theirs
    own = scatter_sum(mine.reshape(chips, mid // chips, neurons_here), "chip")
    mine = share(own, "chip").reshape(mid, neurons_here)
    sketch = mine, other_core(mine)

    core = core.reshape(1)
    rows = lax.all_to_all(gram_rows(core, own, sketch, regions), "region", 0, 0)
    rows = jnp.sum(rows, axis=0)
    mine = share(rows, "chip").reshape(mid, columns)
    gram = mine, other_core(mine)

    gram, signal = lax.optimization_barrier((gram, signal))
    signals = share(signal, "region")
    parts = latent_parts(core, gram, sketch, basis_mix.T, before, activity, regions)
    parts, signals = lax.optimization_barrier((parts, signals))
    latents = scatter_sum((parts * per_unit).astype(jnp.float16), "region")
    latents = share(latents.astype(jnp.float16), "region").astype(full) * unit
    latents_out, frame_sq, stats = error_stats(
        latents, signals, activity, maps, recurrent, bias
    )
    frame_sq = lax.psum(frame_sq.reshape(frames_here), "region")
    stats = stats.reshape((slabs, rank // slabs) + stats.shape[1:])
    stats = share(scatter_sum(stats, SLAB), SLAB)
    stats = stats.reshape((rank,) + stats.shape[2:])
    score = scores(stats, frames_here * slabs)
    return (latents_out, frame_sq / (neurons_here * regions), score.T)


def solution(mesh):
    slabs, regions = mesh.devices.shape
    devices = mesh.devices.reshape(slabs // CORES, CORES, regions)
    mesh = Mesh(devices, ("chip", "core", "region"))
    in_specs = (
        P("region", SLAB),
        P(SLAB, "region"),
        P(),
        P(),
        P(),
        P("region", None),
        P("region", None),
        P("region", None),
        P(),
        P(),
    )
    out_specs = (P(None, SLAB), P(SLAB), P("region", None))
    return jax.shard_map(local, mesh=mesh, in_specs=in_specs, out_specs=out_specs, check_vma=False)
```

```python
import functools

import jax
import jax.numpy as jnp
from jax import lax
from jax.experimental import pallas as pl
from jax.experimental.pallas import tpu as pltpu
from jax.sharding import Mesh
from jax.sharding import PartitionSpec as P

BLOCK = 128
CORES = 2
SLAB = ("chip", "core")

precise = lax.Precision.HIGHEST
epsilon = 1e-05
full = jnp.float32
half = jnp.bfloat16


def product(a, b, ca, cb, precision=None):
    return lax.dot_general(
        a, b, (((ca,), (cb,)), ((), ())), precision=precision, preferred_element_type=full
    )


def other_core(x):
    return lax.ppermute(x, "core", [(0, 1), (1, 0)])


def scatter_sum(pieces, axis):
    return jnp.sum(lax.all_to_all(pieces, axis, 0, 0).astype(full), axis=0)


def share(x, axis):
    copies = jnp.broadcast_to(x[None], (lax.axis_size(axis),) + x.shape)
    return lax.all_to_all(lax.optimization_barrier(copies), axis, 0, 0)


def inverse_factor(tile):
    n = tile.shape[0]
    groups = n // 8
    sub = lax.broadcasted_iota(jnp.int32, (8, n), 0)
    lane = lax.broadcasted_iota(jnp.int32, (8, n), 1)

    def column(x, j):
        return jnp.broadcast_to(x[:, j : j + 1], x.shape)

    def row(x, j):
        return jnp.broadcast_to(x[j : j + 1, :], x.shape)

    left = [tile[8 * q : 8 * q + 8, :] for q in range(groups)]
    right = [jnp.where(lane == sub + 8 * q, full(1), full(0)) for q in range(groups)]
    for p in range(groups):
        at = [column(left[p], 8 * p + j) for j in range(8)]
        lp, rp = left[p], right[p]
        pivots = jnp.ones_like(lp)
        inverse, left_rows, right_rows, pivot_rows = [], [], [], []
        for j in range(8):
            pivot = row(at[j], j)
            pivots = jnp.where(sub == j, pivot, pivots)
            inverse.append(1.0 / pivot)
            left_rows.append(row(lp, j))
            right_rows.append(row(rp, j))
            pivot_rows.append([row(at[k], j) for k in range(j + 1, 8)])
            if j < 7:
                factor = jnp.where(sub > j, at[j] * inverse[j], 0.0)
                for k in range(j + 1, 8):
                    at[k] = at[k] - factor * pivot_rows[j][k - j - 1]
                lp = lp - factor * left_rows[j]
                rp = rp - factor * right_rows[j]
        right[p] = rp * lax.rsqrt(pivots)
        for q in range(p + 1, groups):
            at = [column(left[q], 8 * p + j) for j in range(8)]
            lq, rq = left[q], right[q]
            for j in range(8):
                factor = at[j] * inverse[j]
                for k in range(j + 1, 8):
                    at[k] = at[k] - factor * pivot_rows[j][k - j - 1]
                lq = lq - factor * left_rows[j]
                rq = rq - factor * right_rows[j]
            left[q], right[q] = lq, rq
    return jnp.concatenate(right, axis=0)


def fetch(sources, targets, arrived):
    copies = [
        pltpu.make_async_copy(source, target, arrived.at[i])
        for i, (source, target) in enumerate(zip(sources, targets))
    ]
    for copy in copies:
        copy.start()
    return copies


def latents_kernel(
    core, gram, gram_other, before, sketch, sketch_other, mix, activity,
    out, work, inverse, weights, sketch_here, mix_here, activity_here, arrived,
):
    copies = fetch(
        (sketch, sketch_other, mix, activity),
        (sketch_here.at[0], sketch_here.at[1], mix_here, activity_here),
        arrived,
    )
    n = work.shape[0]
    mid = n // 2
    here = pl.ds(pl.multiple_of(core[0] * mid, mid), mid)
    there = pl.ds(pl.multiple_of((1 - core[0]) * mid, mid), mid)
    work[here, :] = gram[...]
    work[there, :] = gram_other[...]
    starts = range(0, n, BLOCK)
    diagonal = work[:BLOCK, :BLOCK]
    for a in starts:
        e = a + BLOCK
        factor = inverse_factor(diagonal)
        inverse[a:e, :] = factor
        if e < n:
            z = e + BLOCK
            near = product(work[e:z, a:e], factor, 1, 1, precise)
            diagonal = work[e:z, e:z] - product(near, near, 1, 1, precise)
            work[e:z, a:e] = near
        if e < n and z < n:
            far = product(work[z:, a:e], factor, 1, 1, precise)
            work[z:, a:e] = far
            work[z:, e:z] = work[z:, e:z] - product(far, near, 1, 1, precise)
            work[z:, z:] = work[z:, z:] - product(far, far, 1, 1, precise)
    copies[2].wait()
    for a in reversed(starts):
        e = a + BLOCK
        rest = mix_here[:, a:e]
        if e < n:
            rest = rest - product(weights[:, e:], work[e:, a:e], 1, 0, precise)
        weights[:, a:e] = product(rest, inverse[a:e, :], 1, 0, precise)
    copies[0].wait()
    copies[1].wait()
    loading = product(weights[:, here], sketch_here[0], 1, 0, precise)
    loading = loading + product(weights[:, there], sketch_here[1], 1, 0, precise)
    loading = loading.astype(half)
    rank = loading.shape[0]
    pieces, rows, width = out.shape
    prior = product(before[...], loading, 1, 1)
    copies[3].wait()
    for i in range(pieces):
        out[i, :rank, :] = product(
            loading, activity_here[:, i * width : (i + 1) * width], 1, 0
        )
        out[i, rank:, :] = jnp.zeros((rows - rank, width), full)
        out[i, rank:, :rank] = prior[: rows - rank, :]


def in_vmem(count):
    return [pl.BlockSpec(memory_space=pltpu.VMEM)] * count


def anywhere(count):
    return [pl.BlockSpec(memory_space=pl.ANY)] * count


def scalar():
    return pl.BlockSpec(memory_space=pltpu.SMEM)


def gram_kernel(core, own, sketch, sketch_other, out):
    mid = sketch.shape[0]
    mine = product(own[...], sketch[...], 1, 1, precise)
    other = product(own[...], sketch_other[...], 1, 1, precise)
    first = core[0] == 0
    low, high = jnp.where(first, mine, other), jnp.where(first, other, mine)
    for i in range(out.shape[0]):
        out[i, :, :mid] = low
        out[i, :, mid:] = high


def gram_rows(core, own, sketch, copies):
    rows, columns = own.shape[0], 2 * sketch[0].shape[0]
    return pl.pallas_call(
        gram_kernel,
        out_shape=jax.ShapeDtypeStruct((copies, rows, columns), full),
        in_specs=[scalar()] + in_vmem(3),
        out_specs=in_vmem(1)[0],
        compiler_params=pltpu.CompilerParams(vmem_limit_bytes=16 * 2**20),
        cost_estimate=pl.CostEstimate(
            flops=2 * rows * columns * own.shape[1], bytes_accessed=2 * 2**20, transcendentals=0
        ),
        name="gram_rows",
    )(core, own, *sketch)


def signals_kernel(feed, before, marks, activity, out):
    pieces, rows, width = out.shape
    rank = feed.shape[0]
    prior = product(before[...], feed[...], 1, 1)
    upper = lax.broadcasted_iota(jnp.int32, prior.shape, 0) < 8
    prior = jnp.where(upper, prior, marks[...]).astype(half)
    for i in range(pieces):
        signal = product(feed[...], activity[:, i * width : (i + 1) * width], 1, 0)
        out[i, :rank, :] = signal.astype(half)
        out[i, rank:, :] = jnp.zeros((rows - rank, width), half)
        out[i, rank:, :rank] = prior


def signal_parts(feed, before, marks, activity, pieces):
    rank, neurons = feed.shape
    frames = activity.shape[1]
    return pl.pallas_call(
        signals_kernel,
        out_shape=jax.ShapeDtypeStruct((pieces, rank + before.shape[0], frames // pieces), half),
        in_specs=in_vmem(4),
        out_specs=in_vmem(1)[0],
        compiler_params=pltpu.CompilerParams(vmem_limit_bytes=16 * 2**20),
        cost_estimate=pl.CostEstimate(
            flops=2 * rank * neurons * frames, bytes_accessed=4 * 2**20, transcendentals=0
        ),
        name="signal_parts",
    )(feed, before, marks, activity)


def latent_parts(core, gram, sketch, mix, before, activity, pieces):
    n = mix.shape[1]
    rank = mix.shape[0]
    frames = activity.shape[1]
    return pl.pallas_call(
        latents_kernel,
        out_shape=jax.ShapeDtypeStruct((pieces, rank + 8, frames // pieces), full),
        in_specs=[scalar()] + in_vmem(3) + anywhere(4),
        out_specs=in_vmem(1)[0],
        scratch_shapes=[
            pltpu.VMEM((n, n), full),
            pltpu.VMEM((n, BLOCK), full),
            pltpu.VMEM((rank, n), full),
            pltpu.VMEM((2,) + sketch[0].shape, full),
            pltpu.VMEM((rank, n), full),
            pltpu.VMEM(activity.shape, half),
            pltpu.SemaphoreType.DMA((4,)),
        ],
        compiler_params=pltpu.CompilerParams(vmem_limit_bytes=58 * 2**20),
        cost_estimate=pl.CostEstimate(
            flops=2 * n**3, bytes_accessed=8 * 2**20, transcendentals=n
        ),
        name="latent_parts",
    )(core, *gram, before, *sketch, mix, activity)


def lag(block, carry):
    lane = lax.broadcasted_iota(jnp.int32, block.shape, 1)
    return jnp.where(lane == 0, carry, pltpu.roll(block, 1, 1))


def as_column(line):
    n = line.shape[1]
    square = (n, n)
    same = lax.broadcasted_iota(jnp.int32, square, 0) == lax.broadcasted_iota(jnp.int32, square, 1)
    return jnp.sum(jnp.where(same, line, 0.0), axis=1, keepdims=True)


def split(x):
    high = x.astype(half)
    return high, (x - high.astype(full)).astype(half)


def error_kernel(
    latents, signals, activity, maps, recurrent, bias,
    latents_out, frame_out, stats, cross, cross_low, squares, maps_here, arrived,
):
    copies = fetch((maps,), (maps_here,), arrived)
    pieces, _, width = latents.shape
    rank = recurrent.shape[0]
    neurons = activity.shape[0]
    groups = neurons // BLOCK
    last_latent = as_column(latents[0, rank : rank + 1, :rank])
    last_signal = as_column(signals[0, rank : rank + 16, :].astype(full)[:1, :rank])
    hidden_total = jnp.zeros((rank, BLOCK), full)
    for i in range(pieces):
        frames = slice(i * width, (i + 1) * width)
        latent = latents[i, :rank, :]
        signal = signals[i, :rank, :].astype(full)
        latents_out[:, frames] = latent
        lagged_latent = lag(latent, last_latent)
        lagged_signal = lag(signal, last_signal)
        last_latent = latent[:, width - 1 :]
        last_signal = signal[:, width - 1 :]
        hidden = jnp.tanh(product(recurrent[...], lagged_latent, 1, 0, precise) + bias[...])
        high, low = split(hidden)
        state = jnp.concatenate([high, lagged_signal.astype(half)], axis=0)
        both = jnp.concatenate([high, low], axis=0)
        if not i:
            copies[0].wait()
        error = activity[:, frames].astype(full) - product(maps_here[...], state, 1, 0)
        error_high, error_low = split(error)
        by_both = product(error_high, both, 1, 1)
        by_high = product(error_low, high, 1, 1)
        squared = error * error
        frame_out[:, frames] = jnp.sum(squared, axis=0, keepdims=True)
        total = squared[:, :BLOCK]
        hidden_square = hidden * hidden
        for a in range(0, width, BLOCK):
            if a:
                total = total + squared[:, a : a + BLOCK]
            hidden_total = hidden_total + hidden_square[:, a : a + BLOCK]
        if i:
            cross[...] += by_both
            cross_low[...] += by_high
            squares[...] += total
        else:
            cross[...] = by_both
            cross_low[...] = by_high
            squares[...] = total
    error_sq = product(jnp.ones((8, BLOCK), full), squares[...], 1, 1, precise)
    hidden_sq = jnp.sum(hidden_total, axis=1, keepdims=True)
    stats[:, groups:, :] = jnp.zeros((rank, 2, BLOCK), full)
    for g in range(groups):
        lanes = slice(g * BLOCK, (g + 1) * BLOCK)
        by_both = cross[lanes, :].T
        by_high = cross_low[lanes, :].T
        stats[:, g, :] = by_both[:rank, :] + by_both[rank:, :] + by_high
        stats[g, groups + 1 : groups + 2, :] = error_sq[:1, lanes]
    stats[:, groups, :] = jnp.broadcast_to(hidden_sq, (rank, BLOCK))


def error_stats(latents, signals, activity, maps, recurrent, bias):
    neurons, frames = activity.shape
    rank = recurrent.shape[0]
    return pl.pallas_call(
        error_kernel,
        out_shape=(
            jax.ShapeDtypeStruct((rank, frames), full),
            jax.ShapeDtypeStruct((1, frames), full),
            jax.ShapeDtypeStruct((rank, neurons // BLOCK + 2, BLOCK), full),
        ),
        in_specs=in_vmem(3) + anywhere(1) + in_vmem(2),
        out_specs=tuple(in_vmem(3)),
        scratch_shapes=[
            pltpu.VMEM((neurons, 2 * rank), full),
            pltpu.VMEM((neurons, rank), full),
            pltpu.VMEM((neurons, BLOCK), full),
            pltpu.VMEM(maps.shape, half),
            pltpu.SemaphoreType.DMA((1,)),
        ],
        compiler_params=pltpu.CompilerParams(vmem_limit_bytes=40 * 2**20),
        cost_estimate=pl.CostEstimate(
            flops=8 * neurons * frames * rank, bytes_accessed=8 * 2**20, transcendentals=rank * frames
        ),
        name="error_stats",
    )(latents, signals, activity, maps, recurrent, bias)


def score_kernel(frames_all, stats, out):
    groups = stats.shape[1] - 2
    hidden_sq = stats[:, groups, :]
    for g in range(groups):
        lanes = slice(g * BLOCK, (g + 1) * BLOCK)
        error_sq = stats[g, groups + 1 : groups + 2, :]
        out[:, lanes] = stats[:, g, :] / jnp.sqrt(
            frames_all * (error_sq / frames_all + epsilon) * (hidden_sq / frames_all + epsilon)
        )


def scores(stats, frames_all):
    rank, rows, _ = stats.shape
    return pl.pallas_call(
        functools.partial(score_kernel, float(frames_all)),
        out_shape=jax.ShapeDtypeStruct((rank, (rows - 2) * BLOCK), full),
        in_specs=in_vmem(1),
        out_specs=in_vmem(1)[0],
        name="scores",
    )(stats)


def region_tables(block_regions, region_mask, region_in, region_out):
    regions = region_mask.shape[0]
    signal_width = region_in.shape[1]
    block_total = block_regions.shape[0]
    block_rows = region_in.shape[0] // block_total
    onehot = (block_regions[:, None] == jnp.arange(regions, dtype=jnp.int32)[None, :]).astype(full)
    onehot = jnp.broadcast_to(onehot[:, None, :], (block_total, block_rows, regions)).reshape(
        block_total * block_rows, regions
    )
    allowed = jnp.dot(onehot, region_mask.astype(full), precision=precise)
    region_feed = (onehot[:, :, None] * region_in.astype(full)[:, None, :]).reshape(
        -1, regions * signal_width
    )
    spread = (allowed[:, :, None] * region_out.astype(full)[:, None, :]).reshape(
        -1, regions * signal_width
    )
    return (region_feed.astype(half), spread.astype(half))


def local(
    activity,
    test_matrix,
    basis_mix,
    recurrent,
    latent_bias,
    readout,
    region_in,
    region_out,
    region_of_block,
    region_mask,
):
    neurons_here, frames_here = activity.shape
    columns = test_matrix.shape[1] * lax.axis_size("region")
    chips = lax.axis_size("chip")
    slabs = chips * CORES
    regions = lax.axis_size("region")
    core = lax.axis_index("core")

    test_full = lax.all_gather(test_matrix.T, "region", axis=0, tiled=True)
    before = lax.ppermute(activity[:, -1], SLAB, [(i, i + 1) for i in range(slabs - 1)])
    before = jnp.broadcast_to(before[None, :], (16, neurons_here))

    block_count = neurons_here // BLOCK
    my_blocks = lax.dynamic_slice_in_dim(
        region_of_block, lax.axis_index("region") * block_count, block_count
    )
    region_feed, spread = region_tables(my_blocks, region_mask, region_in, region_out)
    maps = jnp.concatenate([readout, spread], axis=1)
    rank = region_feed.shape[1]
    largest = lax.pmax(jnp.max(jnp.abs(test_matrix.astype(full)), axis=0), SLAB)
    here = jnp.arange(16)[:, None] == 8 + lax.axis_index("region")
    marks = jnp.where(here, jnp.pad(largest, (0, rank - largest.shape[0]))[None, :], 0.0)
    signal = signal_parts(region_feed.T, before, marks, activity, regions)
    signal = scatter_sum(signal, "region")
    largest = signal[rank + 8 : rank + 8 + regions, : test_matrix.shape[1]].reshape(columns)
    mid = columns // CORES
    largest = lax.dynamic_slice_in_dim(jnp.maximum(largest, 1e-30), core * mid, mid)
    up = (2 / largest).reshape(chips, mid // chips, 1)
    signal = signal.astype(half)

    largest = jnp.maximum(jnp.max(jnp.abs(basis_mix), axis=0), 1e-30)
    width = frames_here // regions
    unit = jnp.concatenate(
        [
            jnp.broadcast_to(largest[:, None], (rank, width)),
            jnp.broadcast_to(jnp.pad(largest, (0, width - rank), constant_values=1.0), (8, width)),
        ]
    )
    unit = unit / 4
    bias = latent_bias[:, None]
    test_full, signal, maps, before, bias, unit, per_unit, up = lax.optimization_barrier(
        (test_full, signal, maps, before, bias, unit, 1 / unit, up)
    )

    theirs = product(lax.dynamic_slice_in_dim(test_full, (1 - core) * mid, mid), activity, 1, 1)
    theirs = other_core(theirs)
    mine = product(lax.dynamic_slice_in_dim(test_full, core * mid, mid), activity, 1, 1)
    mine = lax.optimization_barrier(mine) + theirs
    mine = mine.reshape(chips, mid // chips, neurons_here) * up
    own = scatter_sum(mine.astype(jnp.float16), "chip") / 26
    own = lax.optimization_barrier(own.astype(jnp.float16))
    mine = share(own, "chip").reshape(mid, neurons_here)
    sketch = mine.astype(full), other_core(mine).astype(full)
    own = own.astype(full)

    core = core.reshape(1)
    rows = lax.all_to_all(gram_rows(core, own, sketch, regions), "region", 0, 0)
    rows = jnp.sum(rows, axis=0)
    mine = share(rows, "chip").reshape(mid, columns)
    gram = mine, other_core(mine)

    gram, signal = lax.optimization_barrier((gram, signal))
    signals = share(signal, "region")
    parts = latent_parts(core, gram, sketch, basis_mix.T, before, activity, regions)
    parts, signals = lax.optimization_barrier((parts, signals))
    latents = scatter_sum((parts * per_unit).astype(jnp.float16), "region")
    latents = share(latents.astype(jnp.float16), "region").astype(full) * unit
    latents_out, frame_sq, stats = error_stats(
        latents, signals, activity, maps, recurrent, bias
    )
    frame_sq = lax.psum(frame_sq.reshape(frames_here), "region")
    stats = stats.reshape((slabs, rank // slabs) + stats.shape[1:])
    stats = share(scatter_sum(stats, SLAB), SLAB)
    stats = stats.reshape((rank,) + stats.shape[2:])
    score = scores(stats, frames_here * slabs)
    return (latents_out, frame_sq / (neurons_here * regions), score.T)


def solution(mesh):
    slabs, regions = mesh.devices.shape
    devices = mesh.devices.reshape(slabs // CORES, CORES, regions)
    mesh = Mesh(devices, ("chip", "core", "region"))
    in_specs = (
        P("region", SLAB),
        P(SLAB, "region"),
        P(),
        P(),
        P(),
        P("region", None),
        P("region", None),
        P("region", None),
        P(),
        P(),
    )
    out_specs = (P(None, SLAB), P(SLAB), P("region", None))
    return jax.shard_map(local, mesh=mesh, in_specs=in_specs, out_specs=out_specs, check_vma=False)
```

```python
import functools

import jax
import jax.numpy as jnp
from jax import lax
from jax.experimental import pallas as pl
from jax.experimental.pallas import tpu as pltpu
from jax.sharding import Mesh
from jax.sharding import PartitionSpec as P

BLOCK = 128
CORES = 2
SLAB = ("chip", "core")

precise = lax.Precision.HIGHEST
epsilon = 1e-05
full = jnp.float32
half = jnp.bfloat16


def product(a, b, ca, cb, precision=None):
    return lax.dot_general(
        a, b, (((ca,), (cb,)), ((), ())), precision=precision, preferred_element_type=full
    )


def other_core(x):
    return lax.ppermute(x, "core", [(0, 1), (1, 0)])


def scatter_sum(pieces, axis):
    return jnp.sum(lax.all_to_all(pieces, axis, 0, 0).astype(full), axis=0)


def share(x, axis):
    copies = jnp.broadcast_to(x[None], (lax.axis_size(axis),) + x.shape)
    return lax.all_to_all(lax.optimization_barrier(copies), axis, 0, 0)


def inverse_factor(tile):
    n = tile.shape[0]
    groups = n // 8
    sub = lax.broadcasted_iota(jnp.int32, (8, n), 0)
    lane = lax.broadcasted_iota(jnp.int32, (8, n), 1)

    def column(x, j):
        return jnp.broadcast_to(x[:, j : j + 1], x.shape)

    def row(x, j):
        return jnp.broadcast_to(x[j : j + 1, :], x.shape)

    left = [tile[8 * q : 8 * q + 8, :] for q in range(groups)]
    right = [jnp.where(lane == sub + 8 * q, full(1), full(0)) for q in range(groups)]
    for p in range(groups):
        at = [column(left[p], 8 * p + j) for j in range(8)]
        lp, rp = left[p], right[p]
        pivots = jnp.ones_like(lp)
        inverse, left_rows, right_rows, pivot_rows = [], [], [], []
        for j in range(8):
            pivot = row(at[j], j)
            pivots = jnp.where(sub == j, pivot, pivots)
            inverse.append(1.0 / pivot)
            left_rows.append(row(lp, j))
            right_rows.append(row(rp, j))
            pivot_rows.append([row(at[k], j) for k in range(j + 1, 8)])
            if j < 7:
                factor = jnp.where(sub > j, at[j] * inverse[j], 0.0)
                for k in range(j + 1, 8):
                    at[k] = at[k] - factor * pivot_rows[j][k - j - 1]
                lp = lp - factor * left_rows[j]
                rp = rp - factor * right_rows[j]
        right[p] = rp * lax.rsqrt(pivots)
        for q in range(p + 1, groups):
            at = [column(left[q], 8 * p + j) for j in range(8)]
            lq, rq = left[q], right[q]
            for j in range(8):
                factor = at[j] * inverse[j]
                for k in range(j + 1, 8):
                    at[k] = at[k] - factor * pivot_rows[j][k - j - 1]
                lq = lq - factor * left_rows[j]
                rq = rq - factor * right_rows[j]
            left[q], right[q] = lq, rq
    return jnp.concatenate(right, axis=0)


def fetch(sources, targets, arrived):
    copies = [
        pltpu.make_async_copy(source, target, arrived.at[i])
        for i, (source, target) in enumerate(zip(sources, targets))
    ]
    for copy in copies:
        copy.start()
    return copies


def latents_kernel(
    core, gram, gram_other, before, sketch, sketch_other, mix, activity,
    out, work, inverse, weights, sketch_here, mix_here, activity_here, arrived,
):
    copies = fetch(
        (sketch, sketch_other, mix, activity),
        (sketch_here.at[0], sketch_here.at[1], mix_here, activity_here),
        arrived,
    )
    n = work.shape[0]
    mid = n // 2
    here = pl.ds(pl.multiple_of(core[0] * mid, mid), mid)
    there = pl.ds(pl.multiple_of((1 - core[0]) * mid, mid), mid)
    work[here, :] = gram[...]
    work[there, :] = gram_other[...]
    starts = range(0, n, BLOCK)
    diagonal = work[:BLOCK, :BLOCK]
    for a in starts:
        e = a + BLOCK
        factor = inverse_factor(diagonal)
        inverse[a:e, :] = factor
        if e < n:
            z = e + BLOCK
            near = product(work[e:z, a:e], factor, 1, 1, precise)
            diagonal = work[e:z, e:z] - product(near, near, 1, 1, precise)
            work[e:z, a:e] = near
        if e < n and z < n:
            far = product(work[z:, a:e], factor, 1, 1, precise)
            work[z:, a:e] = far
            work[z:, e:z] = work[z:, e:z] - product(far, near, 1, 1, precise)
            work[z:, z:] = work[z:, z:] - product(far, far, 1, 1, precise)
    copies[2].wait()
    for a in reversed(starts):
        e = a + BLOCK
        rest = mix_here[:, a:e]
        if e < n:
            rest = rest - product(weights[:, e:], work[e:, a:e], 1, 0, precise)
        weights[:, a:e] = product(rest, inverse[a:e, :], 1, 0, precise)
    copies[0].wait()
    copies[1].wait()
    loading = product(weights[:, here], sketch_here[0], 1, 0, precise)
    loading = loading + product(weights[:, there], sketch_here[1], 1, 0, precise)
    loading = loading.astype(half)
    rank = loading.shape[0]
    pieces, rows, width = out.shape
    prior = product(before[...], loading, 1, 1)
    copies[3].wait()
    for i in range(pieces):
        out[i, :rank, :] = product(
            loading, activity_here[:, i * width : (i + 1) * width], 1, 0
        )
        out[i, rank:, :] = jnp.zeros((rows - rank, width), full)
        out[i, rank:, :rank] = prior[: rows - rank, :]


def in_vmem(count):
    return [pl.BlockSpec(memory_space=pltpu.VMEM)] * count


def anywhere(count):
    return [pl.BlockSpec(memory_space=pl.ANY)] * count


def scalar():
    return pl.BlockSpec(memory_space=pltpu.SMEM)


def gram_kernel(core, own, sketch, sketch_other, out):
    mid = sketch.shape[0]
    mine = product(own[...], sketch[...], 1, 1, precise)
    other = product(own[...], sketch_other[...], 1, 1, precise)
    first = core[0] == 0
    low, high = jnp.where(first, mine, other), jnp.where(first, other, mine)
    for i in range(out.shape[0]):
        out[i, :, :mid] = low
        out[i, :, mid:] = high


def gram_rows(core, own, sketch, copies):
    rows, columns = own.shape[0], 2 * sketch[0].shape[0]
    return pl.pallas_call(
        gram_kernel,
        out_shape=jax.ShapeDtypeStruct((copies, rows, columns), full),
        in_specs=[scalar()] + in_vmem(3),
        out_specs=in_vmem(1)[0],
        compiler_params=pltpu.CompilerParams(vmem_limit_bytes=16 * 2**20),
        cost_estimate=pl.CostEstimate(
            flops=2 * rows * columns * own.shape[1], bytes_accessed=2 * 2**20, transcendentals=0
        ),
        name="gram_rows",
    )(core, own, *sketch)


def signals_kernel(feed, before, marks, activity, out):
    pieces, rows, width = out.shape
    rank = feed.shape[0]
    prior = product(before[...], feed[...], 1, 1)
    upper = lax.broadcasted_iota(jnp.int32, prior.shape, 0) < 8
    prior = jnp.where(upper, prior, marks[...]).astype(half)
    for i in range(pieces):
        signal = product(feed[...], activity[:, i * width : (i + 1) * width], 1, 0)
        out[i, :rank, :] = signal.astype(half)
        out[i, rank:, :] = jnp.zeros((rows - rank, width), half)
        out[i, rank:, :rank] = prior


def signal_parts(feed, before, marks, activity, pieces):
    rank, neurons = feed.shape
    frames = activity.shape[1]
    return pl.pallas_call(
        signals_kernel,
        out_shape=jax.ShapeDtypeStruct((pieces, rank + before.shape[0], frames // pieces), half),
        in_specs=in_vmem(4),
        out_specs=in_vmem(1)[0],
        compiler_params=pltpu.CompilerParams(vmem_limit_bytes=16 * 2**20),
        cost_estimate=pl.CostEstimate(
            flops=2 * rank * neurons * frames, bytes_accessed=4 * 2**20, transcendentals=0
        ),
        name="signal_parts",
    )(feed, before, marks, activity)


def latent_parts(core, gram, sketch, mix, before, activity, pieces):
    n = mix.shape[1]
    rank = mix.shape[0]
    frames = activity.shape[1]
    return pl.pallas_call(
        latents_kernel,
        out_shape=jax.ShapeDtypeStruct((pieces, rank + 8, frames // pieces), full),
        in_specs=[scalar()] + in_vmem(3) + anywhere(4),
        out_specs=in_vmem(1)[0],
        scratch_shapes=[
            pltpu.VMEM((n, n), full),
            pltpu.VMEM((n, BLOCK), full),
            pltpu.VMEM((rank, n), full),
            pltpu.VMEM((2,) + sketch[0].shape, full),
            pltpu.VMEM((rank, n), full),
            pltpu.VMEM(activity.shape, half),
            pltpu.SemaphoreType.DMA((4,)),
        ],
        compiler_params=pltpu.CompilerParams(vmem_limit_bytes=58 * 2**20),
        cost_estimate=pl.CostEstimate(
            flops=2 * n**3, bytes_accessed=8 * 2**20, transcendentals=n
        ),
        name="latent_parts",
    )(core, *gram, before, *sketch, mix, activity)


def lag(block, carry):
    lane = lax.broadcasted_iota(jnp.int32, block.shape, 1)
    return jnp.where(lane == 0, carry, pltpu.roll(block, 1, 1))


def as_column(line):
    n = line.shape[1]
    square = (n, n)
    same = lax.broadcasted_iota(jnp.int32, square, 0) == lax.broadcasted_iota(jnp.int32, square, 1)
    return jnp.sum(jnp.where(same, line, 0.0), axis=1, keepdims=True)


def split(x):
    high = x.astype(half)
    return high, (x - high.astype(full)).astype(half)


def error_kernel(
    latents, signals, activity, maps, recurrent, bias,
    latents_out, frame_out, stats, cross, cross_low, squares, maps_here, arrived,
):
    copies = fetch((maps,), (maps_here,), arrived)
    pieces, _, width = latents.shape
    rank = recurrent.shape[0]
    neurons = activity.shape[0]
    groups = neurons // BLOCK
    last_latent = as_column(latents[0, rank : rank + 1, :rank])
    last_signal = as_column(signals[0, rank : rank + 16, :].astype(full)[:1, :rank])
    hidden_total = jnp.zeros((rank, BLOCK), full)
    for i in range(pieces):
        frames = slice(i * width, (i + 1) * width)
        latent = latents[i, :rank, :]
        signal = signals[i, :rank, :].astype(full)
        latents_out[:, frames] = latent
        lagged_latent = lag(latent, last_latent)
        lagged_signal = lag(signal, last_signal)
        last_latent = latent[:, width - 1 :]
        last_signal = signal[:, width - 1 :]
        hidden = jnp.tanh(product(recurrent[...], lagged_latent, 1, 0, precise) + bias[...])
        high, low = split(hidden)
        state = jnp.concatenate([high, lagged_signal.astype(half)], axis=0)
        both = jnp.concatenate([high, low], axis=0)
        if not i:
            copies[0].wait()
        error = activity[:, frames].astype(full) - product(maps_here[...], state, 1, 0)
        error_high, error_low = split(error)
        by_both = product(error_high, both, 1, 1)
        by_high = product(error_low, high, 1, 1)
        squared = error * error
        frame_out[:, frames] = jnp.sum(squared, axis=0, keepdims=True)
        total = squared[:, :BLOCK]
        hidden_square = hidden * hidden
        for a in range(0, width, BLOCK):
            if a:
                total = total + squared[:, a : a + BLOCK]
            hidden_total = hidden_total + hidden_square[:, a : a + BLOCK]
        if i:
            cross[...] += by_both
            cross_low[...] += by_high
            squares[...] += total
        else:
            cross[...] = by_both
            cross_low[...] = by_high
            squares[...] = total
    error_sq = product(jnp.ones((8, BLOCK), full), squares[...], 1, 1, precise)
    hidden_sq = jnp.sum(hidden_total, axis=1, keepdims=True)
    stats[:, groups:, :] = jnp.zeros((rank, 2, BLOCK), full)
    for g in range(groups):
        lanes = slice(g * BLOCK, (g + 1) * BLOCK)
        by_both = cross[lanes, :].T
        by_high = cross_low[lanes, :].T
        stats[:, g, :] = by_both[:rank, :] + by_both[rank:, :] + by_high
        stats[g, groups + 1 : groups + 2, :] = error_sq[:1, lanes]
    stats[:, groups, :] = jnp.broadcast_to(hidden_sq, (rank, BLOCK))


def error_stats(latents, signals, activity, maps, recurrent, bias):
    neurons, frames = activity.shape
    rank = recurrent.shape[0]
    return pl.pallas_call(
        error_kernel,
        out_shape=(
            jax.ShapeDtypeStruct((rank, frames), full),
            jax.ShapeDtypeStruct((1, frames), full),
            jax.ShapeDtypeStruct((rank, neurons // BLOCK + 2, BLOCK), full),
        ),
        in_specs=in_vmem(3) + anywhere(1) + in_vmem(2),
        out_specs=tuple(in_vmem(3)),
        scratch_shapes=[
            pltpu.VMEM((neurons, 2 * rank), full),
            pltpu.VMEM((neurons, rank), full),
            pltpu.VMEM((neurons, BLOCK), full),
            pltpu.VMEM(maps.shape, half),
            pltpu.SemaphoreType.DMA((1,)),
        ],
        compiler_params=pltpu.CompilerParams(vmem_limit_bytes=40 * 2**20),
        cost_estimate=pl.CostEstimate(
            flops=8 * neurons * frames * rank, bytes_accessed=8 * 2**20, transcendentals=rank * frames
        ),
        name="error_stats",
    )(latents, signals, activity, maps, recurrent, bias)


def score_kernel(frames_all, stats, out):
    groups = stats.shape[1] - 2
    hidden_sq = stats[:, groups, :]
    for g in range(groups):
        lanes = slice(g * BLOCK, (g + 1) * BLOCK)
        error_sq = stats[g, groups + 1 : groups + 2, :]
        out[:, lanes] = stats[:, g, :] / jnp.sqrt(
            frames_all * (error_sq / frames_all + epsilon) * (hidden_sq / frames_all + epsilon)
        )


def scores(stats, frames_all):
    rank, rows, _ = stats.shape
    return pl.pallas_call(
        functools.partial(score_kernel, float(frames_all)),
        out_shape=jax.ShapeDtypeStruct((rank, (rows - 2) * BLOCK), full),
        in_specs=in_vmem(1),
        out_specs=in_vmem(1)[0],
        name="scores",
    )(stats)


def region_tables(block_regions, region_mask, region_in, region_out):
    regions = region_mask.shape[0]
    signal_width = region_in.shape[1]
    block_total = block_regions.shape[0]
    block_rows = region_in.shape[0] // block_total
    onehot = (block_regions[:, None] == jnp.arange(regions, dtype=jnp.int32)[None, :]).astype(full)
    onehot = jnp.broadcast_to(onehot[:, None, :], (block_total, block_rows, regions)).reshape(
        block_total * block_rows, regions
    )
    allowed = jnp.dot(onehot, region_mask.astype(full), precision=precise)
    region_feed = (onehot[:, :, None] * region_in.astype(full)[:, None, :]).reshape(
        -1, regions * signal_width
    )
    spread = (allowed[:, :, None] * region_out.astype(full)[:, None, :]).reshape(
        -1, regions * signal_width
    )
    return (region_feed.astype(half), spread.astype(half))


def local(
    activity,
    test_matrix,
    basis_mix,
    recurrent,
    latent_bias,
    readout,
    region_in,
    region_out,
    region_of_block,
    region_mask,
):
    neurons_here, frames_here = activity.shape
    columns = test_matrix.shape[1] * lax.axis_size("region")
    chips = lax.axis_size("chip")
    slabs = chips * CORES
    regions = lax.axis_size("region")
    core = lax.axis_index("core")

    test_full = lax.all_gather(test_matrix.T, "region", axis=0, tiled=True)
    before = lax.ppermute(activity[:, -1], SLAB, [(i, i + 1) for i in range(slabs - 1)])
    before = jnp.broadcast_to(before[None, :], (16, neurons_here))

    block_count = neurons_here // BLOCK
    my_blocks = lax.dynamic_slice_in_dim(
        region_of_block, lax.axis_index("region") * block_count, block_count
    )
    region_feed, spread = region_tables(my_blocks, region_mask, region_in, region_out)
    maps = jnp.concatenate([readout, spread], axis=1)
    rank = region_feed.shape[1]
    largest = jnp.max(jnp.abs(test_matrix.astype(full)), axis=0)
    block = jnp.pad(largest, (0, BLOCK - largest.shape[0]))
    block = jnp.max(share(jnp.broadcast_to(block[None], (8, BLOCK)), SLAB), axis=0)
    largest = block[0, : largest.shape[0]]
    here = jnp.arange(16)[:, None] == 8 + lax.axis_index("region")
    marks = jnp.where(here, jnp.pad(largest, (0, rank - largest.shape[0]))[None, :], 0.0)
    signal = signal_parts(region_feed.T, before, marks, activity, regions)
    signal = scatter_sum(signal, "region")
    largest = signal[rank + 8 : rank + 8 + regions, : test_matrix.shape[1]].reshape(columns)
    mid = columns // CORES
    largest = lax.dynamic_slice_in_dim(jnp.maximum(largest, 1e-30), core * mid, mid)
    up = (2 / largest).reshape(chips, mid // chips, 1)
    signal = signal.astype(half)

    largest = jnp.maximum(jnp.max(jnp.abs(basis_mix), axis=0), 1e-30)
    width = frames_here // regions
    unit = jnp.concatenate(
        [
            jnp.broadcast_to(largest[:, None], (rank, width)),
            jnp.broadcast_to(jnp.pad(largest, (0, width - rank), constant_values=1.0), (8, width)),
        ]
    )
    unit = unit / 4
    bias = latent_bias[:, None]
    test_full, signal, maps, before, bias, unit, per_unit, up = lax.optimization_barrier(
        (test_full, signal, maps, before, bias, unit, 1 / unit, up)
    )

    theirs = product(lax.dynamic_slice_in_dim(test_full, (1 - core) * mid, mid), activity, 1, 1)
    theirs = other_core(theirs)
    mine = product(lax.dynamic_slice_in_dim(test_full, core * mid, mid), activity, 1, 1)
    mine = lax.optimization_barrier(mine) + theirs
    mine = mine.reshape(chips, mid // chips, neurons_here) * up
    own = scatter_sum(mine.astype(jnp.float16), "chip") / 26
    own = lax.optimization_barrier(own.astype(jnp.float16))
    mine = share(own, "chip").reshape(mid, neurons_here)
    sketch = mine.astype(full), other_core(mine).astype(full)
    own = own.astype(full)

    core = core.reshape(1)
    rows = lax.all_to_all(gram_rows(core, own, sketch, regions), "region", 0, 0)
    rows = jnp.sum(rows, axis=0)
    mine = share(rows, "chip").reshape(mid, columns)
    gram = mine, other_core(mine)

    gram, signal = lax.optimization_barrier((gram, signal))
    signals = share(signal, "region")
    parts = latent_parts(core, gram, sketch, basis_mix.T, before, activity, regions)
    parts, signals = lax.optimization_barrier((parts, signals))
    latents = scatter_sum((parts * per_unit).astype(jnp.float16), "region")
    latents = share(latents.astype(jnp.float16), "region").astype(full) * unit
    latents_out, frame_sq, stats = error_stats(
        latents, signals, activity, maps, recurrent, bias
    )
    frame_sq = lax.psum(frame_sq.reshape(frames_here), "region")
    stats = stats.reshape((slabs, rank // slabs) + stats.shape[1:])
    stats = share(scatter_sum(stats, SLAB), SLAB)
    stats = stats.reshape((rank,) + stats.shape[2:])
    score = scores(stats, frames_here * slabs)
    return (latents_out, frame_sq / (neurons_here * regions), score.T)


def solution(mesh):
    slabs, regions = mesh.devices.shape
    devices = mesh.devices.reshape(slabs // CORES, CORES, regions)
    mesh = Mesh(devices, ("chip", "core", "region"))
    in_specs = (
        P("region", SLAB),
        P(SLAB, "region"),
        P(),
        P(),
        P(),
        P("region", None),
        P("region", None),
        P("region", None),
        P(),
        P(),
    )
    out_specs = (P(None, SLAB), P(SLAB), P("region", None))
    return jax.shard_map(local, mesh=mesh, in_specs=in_specs, out_specs=out_specs, check_vma=False)
```
